32 devices in a mesh: dp: 16 (over z, y, x), expert: 2 (over core).
Axes of the slice: x: 2, y: 2, z: 4, core: 2. Of those that a mesh axis runs over, the one named last changes fastest.
Arguments:
- tokens: bfloat16 [2048, 2048], P('dp'), may hold values from -6 to 6
- arms: int32 [2048], P('dp'), may hold values from 0 to 3
- arm_bias: bfloat16 [4, 2048], replicated, may hold values from -3 to 3
- routes: int32 [2048, 6], P('dp'), may hold values from 0 to 63, all different within a row; in each aligned block of 128 rows (0 to 127, 128 to 255, ...) at most 16 rows name the same one
- gates: int32 [2048, 6], P('dp'), may hold values from 1 to 64
- up_weight: bfloat16 [64, 1408, 2048], P('dp', 'expert'), may hold values from -0.125 to 0.125
- down_weight: bfloat16 [64, 1408, 2048], P('dp', 'expert'), may hold values from -0.15625 to 0.15625
- cotangent: bfloat16 [2048, 2048], P('dp'), may hold values from -1.5 to 1.5
Outputs:
- grad_tokens: float32 [2048, 2048], P('dp', 'expert')
- grad_up: bfloat16 [64, 1408, 2048], P('dp', 'expert')
- grad_down: bfloat16 [64, 1408, 2048], P('dp', 'expert')
The draws below stay inside these ranges and needn't reach their ends.
Inputs may be any that keep to these rules, and one draw needn't show every extreme that they name: The 6 ids of a token differ. Among the routes of the 128 tokens of one index of dp, at most 16 name one expert, and in some such block some expert is named exactly 16 times.
All inputs are finite; a program needn't handle non-finite values.
Results may differ from the reference program's by a relative error of at most 0.014.
Values may be sent and summed in bfloat16 or wider, within the bound.
No kernel may reach another device: no remote copies, remote signals or barrier semaphores. Data moves between devices by JAX's collectives and lax.ppermute only.
A program may use at most 128 MiB of HBM per device.

```python
import math
import jax
import jax.numpy as jnp
import numpy as np
from jax import lax

D = 2048
H = 1408
EXPERTS = 64
TOPK = 6
ARMS = 4
TOK_DEV = 128
CAP = 16
HS = 704
TOKENS = 2048
N_DP = 16
N_EXPERT = 2


def set_ends(result, key, low, largest):
    shape = result.shape
    index_at = [jax.random.randint(jax.random.fold_in(key, axis), (), 0, shape[axis]) for axis in range(len(shape))]
    result = result.at[tuple(index_at)].set(low)
    longest = shape.index(max(shape))
    index_at[longest] = (index_at[longest] + 1) % shape[longest]
    return result.at[tuple(index_at)].set(largest)


def block_scale(own_key, extent, pieces, smallest, largest):
    level, own = 1.0, jax.random.fold_in(own_key, 6)
    for position, blocks in pieces:
        draws = jnp.exp(jax.random.uniform(jax.random.fold_in(own, position), (blocks,), jnp.float32, smallest / len(pieces), largest / len(pieces)))
        level = level * jnp.repeat(draws, extent[position] // blocks).reshape([-1 if axis == position else 1 for axis in range(len(extent))])
    return level


def shared_out(own_key, own, number, rows, count, top, most, skew):
    order = jax.random.permutation(own_key, count)
    packed, common = portions_of(count, rows * top, most, skew, True), portions_of(count, rows * top, most, skew, False)
    places = jnp.arange(count)

    def named(lengths, offset_by):
        used = int((lengths > 0).sum())
        fixed = max(1, used // 4)
        moved = fixed + (places - fixed + offset_by * (used - fixed)) % max(1, count - fixed)
        return jnp.zeros((count,), jnp.int32).at[order[jnp.where(places < fixed, places, moved)]].set(jnp.asarray(lengths, jnp.int32))

    lengths = jnp.where(number % 4 == 0, named(packed, number // 4), named(common, number - number // 4 - 1))
    mixed = jax.random.permutation(jax.random.fold_in(own, 3), count)
    donor, receiver = mixed[0:count // 2 * 2:2], mixed[1:count // 2 * 2:2]
    room = jnp.minimum(lengths[donor] - 1, most - lengths[receiver]) // 2
    room = jnp.where((donor == order[0]) | (receiver == order[0]) | (lengths[receiver] == 0), 0, jnp.maximum(room, 0))
    moved = jax.random.randint(jax.random.fold_in(own, 4), (count // 2,), 0, 1 << 20) % (room + 1)
    lengths = lengths.at[donor].add(-moved).at[receiver].add(moved)
    labels = jnp.searchsorted(jnp.cumsum(lengths), jnp.arange(rows * top), side="right").astype(jnp.int32)
    grid = labels.reshape(top, rows).T
    grid = grid[jax.random.permutation(jax.random.fold_in(own, 1), rows)]
    offset_by = jax.random.randint(jax.random.fold_in(own, 2), (rows, 1), 0, top)
    return jnp.take_along_axis(grid, (jnp.arange(top)[None, :] + offset_by) % top, axis=1)


def portions_of(amount, total, bound, slope, full):
    portions = [(1 << 20) // math.isqrt(standing ** slope) + 1 for standing in range(1, amount + 1)]
    largest = bound if full else min(bound, max(-(-total // amount), total * portions[0] // sum(portions)))
    least = 1 if total - largest >= amount - 1 else 0
    given, rest = [largest] + [least] * (amount - 1), total - largest - least * (amount - 1)
    while rest > 0:
        movable = [i for i in range(1, amount) if given[i] < largest] or [i for i in range(1, amount) if given[i] < bound]
        whole, remaining = sum([portions[i] for i in movable]), rest
        for i in movable:
            extra = min(bound - given[i], max(1, remaining * portions[i] // whole), rest)
            given[i] = given[i] + extra
            rest = rest - extra
    return np.array(given)


def gaussian(key, shape, scale, reach, pieces=(), kind=jnp.bfloat16):
    result = scale * jax.random.normal(key, shape, jnp.float32)
    if pieces:
        result = result * block_scale(key, shape, pieces, -0.22, 0.18)
    return jnp.clip(result, -reach, reach).astype(kind)


def setup_inputs(seed: int = 0) -> dict:
    streams_of = jax.random.split(jax.random.key(seed), 9)
    tokens = gaussian(streams_of[0], (TOKENS, D), 1.0, 6.0, ((0, 16),))
    arms = set_ends(jax.random.randint(streams_of[1], (TOKENS,), 0, ARMS), jax.random.fold_in(streams_of[1], 1), 0, ARMS - 1).astype(jnp.int32)
    arm_bias = gaussian(streams_of[2], (ARMS, D), 0.5, 3.0)
    routes_keys = jax.random.split(jax.random.fold_in(streams_of[3], 1), TOKENS // TOK_DEV)
    routes_turns = jax.random.permutation(jax.random.fold_in(streams_of[3], 3), TOKENS // TOK_DEV)
    routes = jax.vmap(lambda own, number: shared_out(jax.random.fold_in(streams_of[3], 2), own, number, TOK_DEV, EXPERTS, TOPK, CAP, 2))(routes_keys, routes_turns).reshape((TOKENS, TOPK))
    gates = set_ends(jax.random.randint(streams_of[4], (TOKENS, TOPK), 1, 65), jax.random.fold_in(streams_of[4], 1), 1, 64).astype(jnp.int32)
    up_weight = gaussian(streams_of[5], (EXPERTS, H, D), D ** -0.5, 0.125, ((0, 16), (1, 2)))
    down_weight = gaussian(streams_of[6], (EXPERTS, H, D), H ** -0.5, 0.15625, ((0, 16), (1, 2)))
    cotangent = gaussian(streams_of[7], (TOKENS, D), 0.25, 1.5, ((0, 16),))
    return dict(tokens=tokens, arms=arms, arm_bias=arm_bias, routes=routes, gates=gates, up_weight=up_weight, down_weight=down_weight, cotangent=cotangent)


def slot_table(routes):
    flat_ids = routes.reshape(N_DP, TOK_DEV * TOPK).astype(jnp.int32)
    expert_ids = jnp.arange(EXPERTS, dtype=jnp.int32)
    one_hot = (flat_ids[:, :, None] == expert_ids[None, None, :]).astype(jnp.int32)
    rank_table = jnp.cumsum(one_hot, axis=1) - one_hot
    slot_ids = jnp.sum(rank_table * one_hot, axis=2)
    return slot_ids.reshape(-1).astype(jnp.int32)


def reference(tokens, arms, arm_bias, routes, gates, up_weight, down_weight, cotangent):
    lifted = (tokens.astype(jnp.float32) + arm_bias.astype(jnp.float32)[arms]).astype(jnp.bfloat16)
    route_count = TOKENS * TOPK
    flat_routes = routes.reshape(-1).astype(jnp.int32)
    slot_ids = slot_table(routes)
    positions = jnp.arange(route_count, dtype=jnp.int32)
    owner_block = positions // (TOK_DEV * TOPK)
    target_pos = flat_routes * (N_DP * CAP) + owner_block * CAP + slot_ids
    index_table = jnp.full((EXPERTS * N_DP * CAP,), -1, jnp.int32).at[target_pos].set(positions)
    index_table = index_table.reshape(EXPERTS, N_DP * CAP)
    route_weight = gates.reshape(-1).astype(jnp.float32) / 64.0

    def one_expert(running_sum, expert_item):
        row_index, w_up, w_down = expert_item
        live_mask = row_index >= 0
        safe_index = jnp.maximum(row_index, 0)
        token_index = safe_index // TOPK
        expert_rows = jnp.where(live_mask[:, None], lifted[token_index], jnp.zeros((), jnp.bfloat16))
        slot_weight = jnp.where(live_mask, route_weight[safe_index], jnp.zeros((), jnp.float32))
        scaled = (cotangent[token_index].astype(jnp.float32) * slot_weight[:, None]).astype(jnp.bfloat16)
        preact = jnp.dot(expert_rows, w_up.T, preferred_element_type=jnp.float32)
        hidden = jax.nn.silu(preact).astype(jnp.bfloat16)
        backprop = jnp.dot(scaled, w_down.T, preferred_element_type=jnp.float32)
        sigmoid_pre = jax.nn.sigmoid(preact)
        grad_pre = (backprop * sigmoid_pre * (1.0 + preact * (1.0 - sigmoid_pre))).astype(jnp.bfloat16)
        expert_down = jnp.dot(hidden.T, scaled, preferred_element_type=jnp.float32).astype(jnp.bfloat16)
        expert_up = jnp.dot(grad_pre.T, expert_rows, preferred_element_type=jnp.float32).astype(jnp.bfloat16)
        block_terms = jnp.einsum("rsu,sud->rsd", grad_pre.astype(jnp.float32).reshape(-1, N_EXPERT, HS),
                                 w_up.astype(jnp.float32).reshape(N_EXPERT, HS, D)).astype(jnp.bfloat16)
        contrib = jnp.sum(block_terms.astype(jnp.float32), axis=1)
        contrib = jnp.where(live_mask[:, None], contrib, jnp.zeros((), jnp.float32))
        running_sum = running_sum.at[token_index].add(contrib)
        return running_sum, (expert_up, expert_down)

    start_sum = jnp.zeros((TOKENS, D), jnp.float32)
    grad_tokens, (grad_up, grad_down) = lax.scan(one_expert, start_sum, (index_table, up_weight, down_weight))
    return (grad_tokens, grad_up, grad_down)
```

```python
import functools

import jax
import jax.numpy as jnp
from jax import lax
from jax.experimental import pallas as pl
from jax.experimental.pallas import tpu as pltpu
from jax.sharding import PartitionSpec as P

EXPERTS = 64
TOPK = 6
CAP = 16
META = 16
F32 = jnp.float32
BF16 = jnp.bfloat16
VMEM_LIMIT = 48 << 20


def outer_extent(mesh):
    line = list(mesh.devices.reshape(mesh.devices.shape[0], -1)[:, 0])
    total = len(line)
    block = 1
    coords = [getattr(device, "coords", None) for device in line]
    if all(c is not None for c in coords):
        for axis in range(len(coords[0])):
            run = 1
            while run < total and coords[run][axis] == coords[0][axis]:
                run += 1
            if run < total:
                block = max(block, run)
    if block == 1:
        while block * block < total:
            block *= 2
    return total // block


def dot(a, b, dims):
    return lax.dot_general(a, b, (dims, ((), ())), preferred_element_type=F32)


def payload_body(where, tokens, cotangent, meta, bias, out):
    rows = tokens.shape[0]
    arms = meta[2 * TOPK : 2 * TOPK + 1, :].astype(F32)
    ids = lax.broadcasted_iota(jnp.int32, (bias.shape[0], rows), 0).astype(F32)
    pick = (ids == arms).astype(BF16)
    lift = dot(pick, bias[...], ((0,), (0,)))
    out[0:rows, :] = (tokens[...].astype(F32) + lift).astype(BF16)
    out[rows : 2 * rows, :] = cotangent[...]
    out[2 * rows :, :] = jnp.zeros((META, out.shape[1]), BF16)
    out[2 * rows :, 0:rows] = meta[...]


def choose_body(inner, experts_here, where, *refs):
    outs = refs[-(inner + 1) :]
    payloads = refs[: -(inner + 1)]
    table_out = outs[-1]
    rows = (payloads[0].shape[0] - META) // 2
    width = payloads[0].shape[1]
    if len(payloads) == 1:
        load = lambda a, b, c, d: payloads[0][a:b, c:d]
    else:
        flag = where[3] == 1
        load = lambda a, b, c, d: jnp.where(flag, payloads[0][a:b, c:d], payloads[1][a:b, c:d])
    meta = load(2 * rows, 2 * rows + META, 0, rows).astype(F32)
    count = inner * experts_here
    line = lax.broadcasted_iota(jnp.int32, (count, rows), 0)
    owner = jnp.bitwise_xor(lax.div(line, experts_here), where[2])
    ids = ((where[1] * inner + owner) * experts_here + lax.rem(line, experts_here)).astype(F32)
    named = jnp.zeros((count, rows), F32)
    weight = jnp.zeros((count, rows), F32)
    for k in range(TOPK):
        hit = (ids == meta[k : k + 1, :]).astype(F32)
        named = named + hit
        weight = weight + hit * meta[TOPK + k : TOPK + k + 1, :]
    earlier = (
        lax.broadcasted_iota(jnp.int32, (rows, rows), 0) < lax.broadcasted_iota(jnp.int32, (rows, rows), 1)
    ).astype(F32)
    rank = dot(named.astype(BF16), earlier.astype(BF16), ((1,), (0,)))
    rank = jnp.where(named > 0, rank, -1.0)
    slot = lax.broadcasted_iota(jnp.int32, (count, CAP, rows), 1).astype(F32)
    here = slot == rank[:, None, :]
    table = jnp.where(here, 1.0, 0.0).reshape(count * CAP, rows).astype(BF16)
    scale = jnp.where(here, (weight * (1.0 / 64.0))[:, None, :], 0.0).reshape(count * CAP, rows).astype(BF16)
    table_out[...] = table
    lifted = dot(table, load(0, rows, 0, width), ((1,), (0,))).astype(BF16)
    scaled = dot(scale, load(rows, 2 * rows, 0, width), ((1,), (0,))).astype(BF16)
    part = experts_here * CAP
    for m in range(inner):
        outs[m][:, 0:width] = lifted[m * part : (m + 1) * part]
        outs[m][:, width : 2 * width] = scaled[m * part : (m + 1) * part]


def gathered(refs):
    return jnp.concatenate([ref[...].reshape(-1, ref.shape[-1]) for ref in refs], axis=0)


def forward_body(rounds, pieces, where, *refs):
    xs = refs[: rounds * pieces]
    up, hidden_out, slope_out = refs[rounds * pieces :]
    total = None
    for q in range(pieces):
        x = gathered(xs[q * rounds : (q + 1) * rounds])
        width = x.shape[1]
        at = pl.multiple_of(jnp.bitwise_xor(where[0], q) * width, width)
        term = dot(up[0, :, pl.ds(at, width)], x, ((1,), (1,)))
        total = term if total is None else total + term
    s = 1.0 / (1.0 + jnp.exp(-total))
    hidden_out[0] = (total * s).astype(BF16)
    slope_out[0] = s * (1.0 + total * (1.0 - s))


def backward_body(rounds, pieces, where, *refs):
    xs = refs[: rounds * pieces]
    down, up, slope, pre_out = refs[rounds * pieces : rounds * pieces + 4]
    outs = refs[rounds * pieces + 4 :]
    total = None
    for q in range(pieces):
        x = gathered(xs[q * rounds : (q + 1) * rounds])
        width = x.shape[1]
        at = pl.multiple_of(jnp.bitwise_xor(where[0], q) * width, width)
        term = dot(down[0, :, pl.ds(at, width)], x, ((1,), (1,)))
        total = term if total is None else total + term
    pre = (total * slope[0]).astype(BF16)
    pre_out[0] = pre
    for q in range(pieces):
        width = outs[0].shape[-1]
        at = pl.multiple_of(jnp.bitwise_xor(where[0], q) * width, width)
        part = dot(pre, up[0, :, pl.ds(at, width)], ((0,), (0,))).astype(BF16)
        each = part.shape[0] // rounds
        for r in range(rounds):
            ref = outs[q * rounds + r]
            ref[...] = part[r * each : (r + 1) * each].reshape(ref.shape)


def grads_body(rounds, pieces, where, *refs):
    n = rounds * pieces
    lifted, scaled = refs[:n], refs[n : 2 * n]
    hidden, pre, grad_up, grad_down = refs[2 * n :]
    for q in range(pieces):
        width = lifted[0].shape[-1]
        at = pl.multiple_of(jnp.bitwise_xor(where[0], q) * width, width)
        x = gathered(lifted[q * rounds : (q + 1) * rounds])
        grad_up[0, :, pl.ds(at, width)] = dot(pre[0], x, ((1,), (0,))).astype(BF16)
        x = gathered(scaled[q * rounds : (q + 1) * rounds])
        grad_down[0, :, pl.ds(at, width)] = dot(hidden[0], x, ((1,), (0,))).astype(BF16)


def combine_body(blocks, out_dtype, extra, *refs):
    table, out = refs[0], refs[-1]
    rows = jnp.concatenate([ref[...] for ref in refs[1 : 1 + blocks]], axis=0)
    total = dot(table[...], rows, ((0,), (0,)))
    for ref in refs[1 + blocks : 1 + blocks + extra]:
        total = total + ref[...].astype(F32)
    out[...] = total.astype(out_dtype)


def local(outer, tokens, arms, arm_bias, routes, gates, up_weight, down_weight, cotangent):
    count, features = tokens.shape
    here, hidden_width, _ = up_weight.shape
    inner = lax.axis_size("dp") // outer
    pieces = lax.axis_size("expert")
    width = features // pieces
    part = here * CAP
    plane = inner * part
    line = outer * inner * CAP
    dp_index = lax.axis_index("dp")
    core = lax.axis_index("expert")
    z_index = dp_index // inner
    edge = jnp.logical_or(z_index == 0, z_index == outer - 1)
    where = jnp.stack([core, z_index, dp_index % inner, edge.astype(jnp.int32)]).astype(jnp.int32)
    smem = pl.BlockSpec(memory_space=pltpu.SMEM)
    vmem = pl.BlockSpec(memory_space=pltpu.VMEM)
    params = pltpu.CompilerParams(vmem_limit_bytes=VMEM_LIMIT)
    shape = jax.ShapeDtypeStruct

    def cost(flops, moved):
        return pl.CostEstimate(flops=int(flops), bytes_accessed=int(moved), transcendentals=0)

    meta = jnp.concatenate(
        [
            routes.T.astype(BF16),
            gates.T.astype(BF16),
            arms[None, :].astype(BF16),
            jnp.zeros((META - 2 * TOPK - 1, count), BF16),
        ],
        axis=0,
    )
    payload = pl.pallas_call(
        payload_body,
        grid_spec=pltpu.PrefetchScalarGridSpec(
            num_scalar_prefetch=1,
            grid=(1,),
            in_specs=[
                pl.BlockSpec((count, width), lambda i, w: (0, w[0])),
                pl.BlockSpec((count, width), lambda i, w: (0, w[0])),
                pl.BlockSpec((META, count), lambda i, w: (0, 0)),
                pl.BlockSpec((arm_bias.shape[0], width), lambda i, w: (0, w[0])),
            ],
            out_specs=pl.BlockSpec((2 * count + META, width), lambda i, w: (0, 0)),
        ),
        out_shape=shape((2 * count + META, width), BF16),
        compiler_params=params,
        name="payload",
    )(where, tokens, cotangent, meta, arm_bias)

    def across(value, m):
        return lax.ppermute(value, "dp", [(i, i ^ (m * inner)) for i in range(outer * inner)])

    def within(value, m):
        return lax.ppermute(value, "dp", [(i, i ^ m) for i in range(outer * inner)])

    def core_swap(value, q):
        return lax.ppermute(value, "expert", [(i, i ^ q) for i in range(pieces)])

    if outer == 4:
        middle = [(i, i ^ (3 * inner)) for i in range(inner, 3 * inner)]
        outward = [(i, i ^ inner) for i in range(inner, 3 * inner)]
        near = across(payload, 1)
        mid = lax.ppermute(payload, "dp", middle)
        far = lax.ppermute(near, "dp", middle)
        out_mid = lax.ppermute(mid, "dp", outward)
        out_far = lax.ppermute(far, "dp", outward)
        sources = [(payload,), (near,), (out_mid, far), (out_far, mid)]
    else:
        sources = [(payload,)] + [(across(payload, m),) for m in range(1, outer)]

    def choose(candidates):
        outs = pl.pallas_call(
            functools.partial(choose_body, inner, here),
            in_specs=[smem] + [vmem] * len(candidates),
            out_specs=[vmem] * (inner + 1),
            out_shape=[shape((part, 2 * width), BF16)] * inner + [shape((plane, count), BF16)],
            compiler_params=params,
            cost_estimate=cost(4 * plane * count * width, 6 * plane * width),
            name="choose",
        )(where, *candidates)
        return outs[:-1], outs[-1]

    tables, owned = [], []
    for candidates in sources:
        blocks, table = choose(candidates)
        tables.append(table)
        arrived = [blocks[0]] + [within(blocks[m], m) for m in range(1, inner)]
        mine = jnp.concatenate(arrived, axis=0).reshape(inner, here, CAP, 2 * width)
        owned.append([mine] + [core_swap(mine, q) for q in range(1, pieces)])

    rows_in = [owned[r][q] for q in range(pieces) for r in range(outer)]
    n_in = len(rows_in)
    lifted_spec = [pl.BlockSpec((inner, 1, CAP, width), lambda e: (0, e, 0, 0))] * n_in
    scaled_spec = [pl.BlockSpec((inner, 1, CAP, width), lambda e: (0, e, 0, 1))] * n_in
    weight_spec = pl.BlockSpec((1, hidden_width, features), lambda e: (e, 0, 0))
    unit_spec = pl.BlockSpec((1, hidden_width, line), lambda e: (e, 0, 0))
    weight_bytes = 2 * here * hidden_width * features
    row_bytes = 2 * here * line * features
    flops = 2 * here * line * hidden_width * features
    unit_shape = (here, hidden_width, line)
    hidden, slope = pl.pallas_call(
        functools.partial(forward_body, outer, pieces),
        grid=(here,),
        in_specs=[smem] + lifted_spec + [weight_spec],
        out_specs=[unit_spec, unit_spec],
        out_shape=[shape(unit_shape, BF16), shape(unit_shape, F32)],
        compiler_params=params,
        cost_estimate=cost(flops, weight_bytes + row_bytes),
        name="forward",
    )(where, *rows_in, up_weight)
    back = pl.pallas_call(
        functools.partial(backward_body, outer, pieces),
        grid=(here,),
        in_specs=[smem] + scaled_spec + [weight_spec, weight_spec, unit_spec],
        out_specs=[unit_spec] + lifted_spec,
        out_shape=[shape(unit_shape, BF16)] + [shape((inner, here, CAP, width), BF16)] * n_in,
        compiler_params=params,
        cost_estimate=cost(2 * flops, 2 * weight_bytes + 2 * row_bytes),
        name="backward",
    )(where, *rows_in, down_weight, up_weight, slope)
    pre, partial = back[0], back[1:]
    grad_up, grad_down = pl.pallas_call(
        functools.partial(grads_body, outer, pieces),
        grid=(here,),
        in_specs=[smem] + lifted_spec + scaled_spec + [unit_spec, unit_spec],
        out_specs=[weight_spec, weight_spec],
        out_shape=[shape(up_weight.shape, BF16)] * 2,
        compiler_params=params,
        cost_estimate=cost(2 * flops, 2 * weight_bytes + 2 * row_bytes),
        name="grads",
    )(where, *rows_in, *rows_in, hidden, pre)

    def combine(r, blocks, extra, dtype):
        return pl.pallas_call(
            functools.partial(combine_body, len(blocks), dtype, len(extra)),
            in_specs=[vmem] * (1 + len(blocks) + len(extra)),
            out_specs=vmem,
            out_shape=shape((count, width), dtype),
            compiler_params=params,
            cost_estimate=cost(2 * plane * count * width, 2 * plane * width),
            name="combine",
        )(tables[r], *blocks, *extra)

    sums = []
    for r in reversed(range(outer)):
        total = partial[r].astype(F32)
        for q in range(1, pieces):
            total = total + core_swap(partial[q * outer + r], q).astype(F32)
        ready = total.astype(BF16).reshape(inner, part, width)
        blocks = [ready[0]] + [within(ready[m], m) for m in range(1, inner)]
        if r:
            sums.append(across(combine(r, blocks, [], BF16), r))
        else:
            grad_tokens = combine(0, blocks, sums, F32)
    return (grad_tokens, grad_up, grad_down)


def solution(mesh):
    in_specs = (
        P("dp", None),
        P("dp"),
        P(),
        P("dp", None),
        P("dp", None),
        P("dp", "expert", None),
        P("dp", "expert", None),
        P("dp", None),
    )
    out_specs = (P("dp", "expert"), P("dp", "expert", None), P("dp", "expert", None))
    return jax.shard_map(
        functools.partial(local, outer_extent(mesh)), mesh=mesh, in_specs=in_specs, out_specs=out_specs, check_vma=False
    )
```

```python
import functools

import jax
import jax.numpy as jnp
from jax import lax
from jax.experimental import pallas as pl
from jax.experimental.pallas import tpu as pltpu
from jax.sharding import PartitionSpec as P

EXPERTS = 64
TOPK = 6
CAP = 16
META = 16
F32 = jnp.float32
BF16 = jnp.bfloat16
VMEM_LIMIT = 32 << 20
PAYLOAD_LIMIT = 62 << 20


def outer_extent(mesh):
    line = list(mesh.devices.reshape(mesh.devices.shape[0], -1)[:, 0])
    total = len(line)
    block = 1
    coords = [getattr(device, "coords", None) for device in line]
    if all(c is not None for c in coords):
        for axis in range(len(coords[0])):
            run = 1
            while run < total and coords[run][axis] == coords[0][axis]:
                run += 1
            if run < total:
                block = max(block, run)
    if block == 1:
        while block * block < total:
            block *= 2
    return total // block


def dot(a, b, dims):
    return lax.dot_general(a, b, (dims, ((), ())), preferred_element_type=F32)


def payload_body(where, routes, gates, arms, tokens, cotangent, bias, out, rows_in, bias_in, sems):
    rows, width = rows_in.shape[1:]
    at = pl.multiple_of(where[0] * width, width)
    copies = [
        pltpu.make_async_copy(tokens.at[:, pl.ds(at, width)], rows_in.at[0], sems.at[0]),
        pltpu.make_async_copy(cotangent.at[:, pl.ds(at, width)], rows_in.at[1], sems.at[1]),
        pltpu.make_async_copy(bias.at[:, pl.ds(at, width)], bias_in, sems.at[2]),
    ]
    for copy in copies:
        copy.start()
    ids = lax.broadcasted_iota(jnp.int32, (bias.shape[0], rows), 0)
    pick = (ids == arms[...]).astype(F32).astype(BF16)
    out[2 * rows :, :] = jnp.zeros((META, width), BF16)
    table = [ref[...].astype(F32) for ref in (routes, gates)]
    rest = jnp.zeros((META - 2 * TOPK, rows), F32)
    out[2 * rows :, 0:rows] = jnp.concatenate(table + [rest], axis=0).astype(BF16)
    for copy in copies:
        copy.wait()
    lift = dot(pick, bias_in[...], ((0,), (0,)))
    out[0:rows, :] = (rows_in[0].astype(F32) + lift).astype(BF16)
    out[rows : 2 * rows, :] = rows_in[1]


def choose_body(inner, experts_here, where, *refs):
    outs = refs[-(inner + 1) :]
    payloads = refs[: -(inner + 1)]
    table_out = outs[-1]
    rows = (payloads[0].shape[0] - META) // 2
    width = payloads[0].shape[1]
    if len(payloads) == 1:
        load = lambda a, b, c, d: payloads[0][a:b, c:d]
    else:
        flag = where[3] == 1
        load = lambda a, b, c, d: jnp.where(flag, payloads[0][a:b, c:d], payloads[1][a:b, c:d])
    meta = load(2 * rows, 2 * rows + META, 0, rows).astype(F32)
    count = inner * experts_here
    line = lax.broadcasted_iota(jnp.int32, (count, rows), 0)
    owner = jnp.bitwise_xor(lax.div(line, experts_here), where[2])
    ids = ((where[1] * inner + owner) * experts_here + lax.rem(line, experts_here)).astype(F32)
    named = jnp.zeros((count, rows), F32)
    weight = jnp.zeros((count, rows), F32)
    for k in range(TOPK):
        hit = (ids == meta[k : k + 1, :]).astype(F32)
        named = named + hit
        weight = weight + hit * meta[TOPK + k : TOPK + k + 1, :]
    earlier = (
        lax.broadcasted_iota(jnp.int32, (rows, rows), 0) < lax.broadcasted_iota(jnp.int32, (rows, rows), 1)
    ).astype(F32)
    rank = dot(named.astype(BF16), earlier.astype(BF16), ((1,), (0,)))
    rank = jnp.where(named > 0, rank, -1.0)
    slot = lax.broadcasted_iota(jnp.int32, (count, CAP, rows), 1).astype(F32)
    here = slot == rank[:, None, :]
    table = jnp.where(here, 1.0, 0.0).reshape(count * CAP, rows).astype(BF16)
    scale = jnp.where(here, (weight * (1.0 / 64.0))[:, None, :], 0.0).reshape(count * CAP, rows).astype(BF16)
    table_out[...] = table
    lifted = dot(table, load(0, rows, 0, width), ((1,), (0,))).astype(BF16)
    scaled = dot(scale, load(rows, 2 * rows, 0, width), ((1,), (0,))).astype(BF16)
    part = experts_here * CAP
    for m in range(inner):
        outs[m][:, 0:width] = lifted[m * part : (m + 1) * part]
        outs[m][:, width : 2 * width] = scaled[m * part : (m + 1) * part]


def gathered(refs):
    return jnp.concatenate([ref[...].reshape(-1, ref.shape[-1]) for ref in refs], axis=0)


def rows_body(rounds, pieces, where, *refs):
    n = rounds * pieces
    lifted, scaled = refs[:n], refs[n : 2 * n]
    up, down, hidden_out, pre_out = refs[2 * n : 2 * n + 4]
    outs = refs[2 * n + 4 :]
    width = outs[0].shape[-1]
    at = [pl.multiple_of(jnp.bitwise_xor(where[0], q) * width, width) for q in range(pieces)]

    def project(weight, xs):
        total = None
        for q in range(pieces):
            term = dot(weight[0, :, pl.ds(at[q], width)], gathered(xs[q * rounds : (q + 1) * rounds]), ((1,), (1,)))
            total = term if total is None else total + term
        return total

    preact = project(up, lifted)
    backprop = project(down, scaled)
    s = 1.0 / (1.0 + jnp.exp(-preact))
    hidden_out[0] = (preact * s).astype(BF16)
    pre = (backprop * s * (1.0 + preact * (1.0 - s))).astype(BF16)
    pre_out[0] = pre
    turned = pre.T
    for q in range(pieces):
        part = dot(turned, up[0, :, pl.ds(at[q], width)], ((1,), (0,))).astype(BF16)
        each = part.shape[0] // rounds
        for r in range(rounds):
            ref = outs[q * rounds + r]
            ref[...] = part[r * each : (r + 1) * each].reshape(ref.shape)


def grads_body(rounds, pieces, where, *refs):
    n = rounds * pieces
    hidden, pre, grad_up, grad_down, flag = refs[2 * n :]
    for unit, xs, grad in ((pre, refs[:n], grad_up), (hidden, refs[n : 2 * n], grad_down)):
        for q in range(pieces):
            width = xs[0].shape[-1]
            at = pl.multiple_of(jnp.bitwise_xor(where[0], q) * width, width)
            x = gathered(xs[q * rounds : (q + 1) * rounds])
            grad[0, :, pl.ds(at, width)] = dot(unit[0], x, ((1,), (0,))).astype(BF16)
    flag[...] = jnp.zeros(flag.shape, F32)


def combine_body(blocks, out_dtype, extra, *refs):
    table, out = refs[0], refs[-1]
    rows = jnp.concatenate([ref[...] for ref in refs[1 : 1 + blocks]], axis=0)
    total = dot(table[...], rows, ((0,), (0,)))
    for ref in refs[1 + blocks : 1 + blocks + extra]:
        total = total + ref[...].astype(F32)
    out[...] = total.astype(out_dtype)


def local(outer, tokens, arms, arm_bias, routes, gates, up_weight, down_weight, cotangent):
    count, features = tokens.shape
    here, hidden_width, _ = up_weight.shape
    inner = lax.axis_size("dp") // outer
    pieces = lax.axis_size("expert")
    width = features // pieces
    part = here * CAP
    plane = inner * part
    line = outer * inner * CAP
    dp_index = lax.axis_index("dp")
    core = lax.axis_index("expert")
    z_index = dp_index // inner
    edge = jnp.logical_or(z_index == 0, z_index == outer - 1)
    where = jnp.stack([core, z_index, dp_index % inner, edge.astype(jnp.int32)]).astype(jnp.int32)
    smem = pl.BlockSpec(memory_space=pltpu.SMEM)
    vmem = pl.BlockSpec(memory_space=pltpu.VMEM)
    params = pltpu.CompilerParams(vmem_limit_bytes=VMEM_LIMIT)
    shape = jax.ShapeDtypeStruct

    def cost(flops, moved):
        return pl.CostEstimate(flops=int(flops), bytes_accessed=int(moved), transcendentals=0)

    hbm = pl.BlockSpec(memory_space=pltpu.HBM)
    payload = pl.pallas_call(
        payload_body,
        in_specs=[smem, vmem, vmem, vmem, hbm, hbm, hbm],
        out_specs=vmem,
        out_shape=shape((2 * count + META, width), BF16),
        scratch_shapes=[
            pltpu.VMEM((2, count, width), BF16),
            pltpu.VMEM((arm_bias.shape[0], width), BF16),
            pltpu.SemaphoreType.DMA((3,)),
        ],
        compiler_params=pltpu.CompilerParams(vmem_limit_bytes=PAYLOAD_LIMIT),
        name="payload",
    )(where, routes.T, gates.T, arms.reshape(1, count), tokens, cotangent, arm_bias)

    def across(value, m):
        return lax.ppermute(value, "dp", [(i, i ^ (m * inner)) for i in range(outer * inner)])

    def within(value, m):
        return lax.ppermute(value, "dp", [(i, i ^ m) for i in range(outer * inner)])

    def core_swap(value, q):
        return lax.ppermute(value, "expert", [(i, i ^ q) for i in range(pieces)])

    def choose(candidates):
        outs = pl.pallas_call(
            functools.partial(choose_body, inner, here),
            in_specs=[smem] + [vmem] * len(candidates),
            out_specs=[vmem] * (inner + 1),
            out_shape=[shape((part, 2 * width), BF16)] * inner + [shape((plane, count), BF16)],
            compiler_params=params,
            cost_estimate=cost(4 * plane * count * width, 6 * plane * width),
            name="choose",
        )(where, *candidates)
        return outs[:-1], outs[-1]

    def after(value, *others):
        return lax.optimization_barrier((value, *others))[0]

    tables, owned = [], []

    def spread(blocks):
        return [blocks[0]] + [within(blocks[m], m) for m in range(1, inner)]

    def share(arrived):
        mine = jnp.concatenate(arrived, axis=0).reshape(inner, here, CAP, 2 * width)
        owned.append([mine] + [core_swap(mine, q) for q in range(1, pieces)])

    def pick(candidates):
        blocks, table = choose(candidates)
        tables.append(table)
        return blocks

    if outer == 4:
        middle = [(i, i ^ (3 * inner)) for i in range(inner, 3 * inner)]
        outward = [(i, i ^ inner) for i in range(inner, 3 * inner)]
        near = across(payload, 1)
        mid = lax.ppermute(payload, "dp", middle)
        first = spread(pick((payload,)))
        second = pick((near,))
        near, mid, first, second = lax.optimization_barrier((near, mid, first, second))
        share(first)
        far = lax.ppermute(near, "dp", middle)
        out_mid = lax.ppermute(mid, "dp", outward)
        second = spread(second)
        third = pick((out_mid, far))
        far, second, third = lax.optimization_barrier((far, second, third))
        share(second)
        out_far = lax.ppermute(far, "dp", outward)
        third = spread(third)
        fourth = pick((out_far, mid))
        third, fourth = lax.optimization_barrier((third, fourth))
        share(third)
        share(spread(fourth))
    else:
        for m in range(outer):
            share(spread(pick((across(payload, m) if m else payload,))))

    rows_in = [owned[r][q] for q in range(pieces) for r in range(outer)]
    n_in = len(rows_in)
    lifted_spec = [pl.BlockSpec((inner, 1, CAP, width), lambda e: (0, e, 0, 0))] * n_in
    scaled_spec = [pl.BlockSpec((inner, 1, CAP, width), lambda e: (0, e, 0, 1))] * n_in
    weight_spec = pl.BlockSpec((1, hidden_width, features), lambda e: (e, 0, 0))
    unit_spec = pl.BlockSpec((1, hidden_width, line), lambda e: (e, 0, 0))
    weight_bytes = 2 * here * hidden_width * features
    row_bytes = 2 * here * line * features
    flops = 2 * here * line * hidden_width * features
    unit_shape = (here, hidden_width, line)
    back = pl.pallas_call(
        functools.partial(rows_body, outer, pieces),
        grid=(here,),
        in_specs=[smem] + lifted_spec + scaled_spec + [weight_spec, weight_spec],
        out_specs=[unit_spec, unit_spec] + lifted_spec,
        out_shape=[shape(unit_shape, BF16)] * 2 + [shape((inner, here, CAP, width), BF16)] * n_in,
        compiler_params=params,
        cost_estimate=cost(3 * flops, 2 * weight_bytes + 3 * row_bytes),
        name="rows",
    )(where, *rows_in, *rows_in, up_weight, down_weight)
    hidden, pre, partial = back[0], back[1], back[2:]
    def weight_grads(ordered):
        return pl.pallas_call(
            functools.partial(grads_body, outer, pieces),
            grid=(here,),
            in_specs=[smem] + lifted_spec + scaled_spec + [unit_spec, unit_spec],
            out_specs=[weight_spec, weight_spec, pl.BlockSpec((8, 128), lambda e: (0, 0))],
            out_shape=[shape(up_weight.shape, BF16)] * 2 + [shape((8, 128), F32)],
            compiler_params=params,
            cost_estimate=cost(2 * flops, 2 * weight_bytes + 2 * row_bytes),
            name="weight_grads",
        )(ordered, *rows_in, *rows_in, hidden, pre)

    def combine(r, blocks, extra, dtype):
        return pl.pallas_call(
            functools.partial(combine_body, len(blocks), dtype, len(extra)),
            in_specs=[vmem] * (1 + len(blocks) + len(extra)),
            out_specs=vmem,
            out_shape=shape((count, width), dtype),
            compiler_params=params,
            cost_estimate=cost(2 * plane * count * width, 2 * plane * width),
            name="combine",
        )(tables[r], *blocks, *extra)

    sums = []
    swapped = [[core_swap(partial[q * outer + r], q) for q in range(1, pieces)] for r in range(outer)]
    ready = [None] * outer
    for r in range(outer):
        total = partial[r].astype(F32)
        for value in swapped[r]:
            total = total + value.astype(F32)
        ready[r] = total.astype(BF16).reshape(inner, part, width)
    grad_up, grad_down, flag = weight_grads(where)
    for r in reversed(range(outer)):
        blocks = [ready[r][0]] + [within(ready[r][m], m) for m in range(1, inner)]
        if r:
            blocks[-1], ready[r - 1] = lax.optimization_barrier((blocks[-1], ready[r - 1]))
            sums.append(across(combine(r, blocks, [], BF16), r))
        else:
            grad_tokens = combine(0, blocks, sums, F32)
    return (grad_tokens, grad_up, grad_down)


def solution(mesh):
    in_specs = (
        P("dp", None),
        P("dp"),
        P(),
        P("dp", None),
        P("dp", None),
        P("dp", "expert", None),
        P("dp", "expert", None),
        P("dp", None),
    )
    out_specs = (P("dp", "expert"), P("dp", "expert", None), P("dp", "expert", None))
    return jax.shard_map(
        functools.partial(local, outer_extent(mesh)), mesh=mesh, in_specs=in_specs, out_specs=out_specs, check_vma=False
    )
```

```python
import functools

import jax
import jax.numpy as jnp
from jax import lax
from jax.experimental import pallas as pl
from jax.experimental.pallas import tpu as pltpu
from jax.sharding import PartitionSpec as P

EXPERTS = 64
TOPK = 6
CAP = 16
META = 16
F32 = jnp.float32
BF16 = jnp.bfloat16
VMEM_LIMIT = 32 << 20
PAYLOAD_LIMIT = 62 << 20


def outer_extent(mesh):
    line = list(mesh.devices.reshape(mesh.devices.shape[0], -1)[:, 0])
    total = len(line)
    block = 1
    coords = [getattr(device, "coords", None) for device in line]
    if all(c is not None for c in coords):
        for axis in range(len(coords[0])):
            run = 1
            while run < total and coords[run][axis] == coords[0][axis]:
                run += 1
            if run < total:
                block = max(block, run)
    if block == 1:
        while block * block < total:
            block *= 2
    return total // block


def dot(a, b, dims):
    return lax.dot_general(a, b, (dims, ((), ())), preferred_element_type=F32)


def payload_body(inner, experts_here, routes, gates, arms, tokens, cotangent, bias, out, *refs):
    rows_in, bias_in, sems = refs[inner + 1 :]
    dp_index = lax.axis_index("dp")
    where = [lax.axis_index("expert"), lax.div(dp_index, inner), lax.rem(dp_index, inner)]
    rows, width = rows_in.shape[1:]
    at = pl.multiple_of(where[0] * width, width)
    copies = [
        pltpu.make_async_copy(tokens.at[:, pl.ds(at, width)], rows_in.at[0], sems.at[0]),
        pltpu.make_async_copy(cotangent.at[:, pl.ds(at, width)], rows_in.at[1], sems.at[1]),
        pltpu.make_async_copy(bias.at[:, pl.ds(at, width)], bias_in, sems.at[2]),
    ]
    for copy in copies:
        copy.start()
    ids = lax.broadcasted_iota(jnp.int32, (bias.shape[0], rows), 0)
    pick = (ids == arms[...]).astype(F32).astype(BF16)
    out[2 * rows :, :] = jnp.zeros((META, width), BF16)
    table = [ref[...].astype(F32) for ref in (routes, gates)]
    rest = jnp.zeros((META - 2 * TOPK, rows), F32)
    out[2 * rows :, 0:rows] = jnp.concatenate(table + [rest], axis=0).astype(BF16)
    for copy in copies:
        copy.wait()
    lift = dot(pick, bias_in[...], ((0,), (0,)))
    out[0:rows, :] = (rows_in[0].astype(F32) + lift).astype(BF16)
    out[rows : 2 * rows, :] = rows_in[1]
    choose_body(inner, experts_here, where, out, *refs[: inner + 1])


def choose_body(inner, experts_here, where, *refs):
    outs = refs[-(inner + 1) :]
    payloads = refs[: -(inner + 1)]
    table_out = outs[-1]
    rows = (payloads[0].shape[0] - META) // 2
    width = payloads[0].shape[1]
    if len(payloads) == 1:
        load = lambda a, b, c, d: payloads[0][a:b, c:d]
    else:
        flag = where[3] == 1
        load = lambda a, b, c, d: jnp.where(flag, payloads[0][a:b, c:d], payloads[1][a:b, c:d])
    meta = load(2 * rows, 2 * rows + META, 0, rows).astype(F32)
    count = inner * experts_here
    line = lax.broadcasted_iota(jnp.int32, (count, rows), 0)
    owner = jnp.bitwise_xor(lax.div(line, experts_here), where[2])
    ids = ((where[1] * inner + owner) * experts_here + lax.rem(line, experts_here)).astype(F32)
    named = jnp.zeros((count, rows), F32)
    weight = jnp.zeros((count, rows), F32)
    for k in range(TOPK):
        hit = (ids == meta[k : k + 1, :]).astype(F32)
        named = named + hit
        weight = weight + hit * meta[TOPK + k : TOPK + k + 1, :]
    earlier = (
        lax.broadcasted_iota(jnp.int32, (rows, rows), 0) < lax.broadcasted_iota(jnp.int32, (rows, rows), 1)
    ).astype(F32)
    rank = dot(named.astype(BF16), earlier.astype(BF16), ((1,), (0,)))
    rank = jnp.where(named > 0, rank, -1.0)
    slot = lax.broadcasted_iota(jnp.int32, (count, CAP, rows), 1).astype(F32)
    here = slot == rank[:, None, :]
    table = jnp.where(here, 1.0, 0.0).reshape(count * CAP, rows).astype(BF16)
    scale = jnp.where(here, (weight * (1.0 / 64.0))[:, None, :], 0.0).reshape(count * CAP, rows).astype(BF16)
    table_out[...] = table
    lifted = dot(table, load(0, rows, 0, width), ((1,), (0,))).astype(BF16)
    scaled = dot(scale, load(rows, 2 * rows, 0, width), ((1,), (0,))).astype(BF16)
    part = experts_here * CAP
    for m in range(inner):
        outs[m][:, 0:width] = lifted[m * part : (m + 1) * part]
        outs[m][:, width : 2 * width] = scaled[m * part : (m + 1) * part]


def gathered(refs):
    return jnp.concatenate([ref[...].reshape(-1, ref.shape[-1]) for ref in refs], axis=0)


def rows_body(rounds, pieces, where, *refs):
    n = rounds * pieces
    lifted, scaled = refs[:n], refs[n : 2 * n]
    up, down, hidden_out, pre_out = refs[2 * n : 2 * n + 4]
    outs = refs[2 * n + 4 :]
    width = outs[0].shape[-1]
    at = [pl.multiple_of(jnp.bitwise_xor(where[0], q) * width, width) for q in range(pieces)]

    def project(weight, xs):
        total = None
        for q in range(pieces):
            term = dot(weight[0, :, pl.ds(at[q], width)], gathered(xs[q * rounds : (q + 1) * rounds]), ((1,), (1,)))
            total = term if total is None else total + term
        return total

    preact = project(up, lifted)
    backprop = project(down, scaled)
    s = 1.0 / (1.0 + jnp.exp(-preact))
    hidden_out[0] = (preact * s).astype(BF16)
    pre = (backprop * s * (1.0 + preact * (1.0 - s))).astype(BF16)
    pre_out[0] = pre
    turned = pre.T
    for q in range(pieces):
        part = dot(turned, up[0, :, pl.ds(at[q], width)], ((1,), (0,))).astype(BF16)
        each = part.shape[0] // rounds
        for r in range(rounds):
            ref = outs[q * rounds + r]
            ref[...] = part[r * each : (r + 1) * each].reshape(ref.shape)


def grads_body(rounds, pieces, where, *refs):
    n = rounds * pieces
    hidden, pre, _, grad_up, grad_down, flag = refs[2 * n :]
    for unit, xs, grad in ((pre, refs[:n], grad_up), (hidden, refs[n : 2 * n], grad_down)):
        for q in range(pieces):
            width = xs[0].shape[-1]
            at = pl.multiple_of(jnp.bitwise_xor(where[0], q) * width, width)
            x = gathered(xs[q * rounds : (q + 1) * rounds])
            grad[0, :, pl.ds(at, width)] = dot(unit[0], x, ((1,), (0,))).astype(BF16)
    flag[...] = jnp.zeros(flag.shape, F32)


def combine_body(blocks, groups, *refs):
    tables, rows, outs = refs[:groups], refs[groups : groups + blocks], refs[-groups:]
    part = rows[0].shape[0] // groups
    for g in range(groups):
        mine = jnp.concatenate([ref[g * part : (g + 1) * part, :] for ref in rows], axis=0)
        outs[g][...] = dot(tables[g][...], mine, ((0,), (0,))).astype(outs[g].dtype)


def local(outer, tokens, arms, arm_bias, routes, gates, up_weight, down_weight, cotangent):
    count, features = tokens.shape
    here, hidden_width, _ = up_weight.shape
    inner = lax.axis_size("dp") // outer
    pieces = lax.axis_size("expert")
    width = features // pieces
    part = here * CAP
    plane = inner * part
    line = outer * inner * CAP
    dp_index = lax.axis_index("dp")
    core = lax.axis_index("expert")
    z_index = dp_index // inner
    edge = jnp.logical_or(z_index == 0, z_index == outer - 1)
    where = jnp.stack([core, z_index, dp_index % inner, edge.astype(jnp.int32)]).astype(jnp.int32)
    smem = pl.BlockSpec(memory_space=pltpu.SMEM)
    vmem = pl.BlockSpec(memory_space=pltpu.VMEM)
    params = pltpu.CompilerParams(vmem_limit_bytes=VMEM_LIMIT)
    shape = jax.ShapeDtypeStruct

    def cost(flops, moved):
        return pl.CostEstimate(flops=int(flops), bytes_accessed=int(moved), transcendentals=0)

    hbm = pl.BlockSpec(memory_space=pltpu.HBM)
    chosen_shape = [shape((part, 2 * width), BF16)] * inner + [shape((plane, count), BF16)]
    payload, *own = pl.pallas_call(
        functools.partial(payload_body, inner, here),
        in_specs=[vmem, vmem, vmem, hbm, hbm, hbm],
        out_specs=[vmem] * (inner + 2),
        out_shape=[shape((2 * count + META, width), BF16), *chosen_shape],
        scratch_shapes=[
            pltpu.VMEM((2, count, width), BF16),
            pltpu.VMEM((arm_bias.shape[0], width), BF16),
            pltpu.SemaphoreType.DMA((3,)),
        ],
        compiler_params=pltpu.CompilerParams(vmem_limit_bytes=PAYLOAD_LIMIT),
        name="payload",
    )(routes.T, gates.T, arms.reshape(1, count), tokens, cotangent, arm_bias)

    def across(value, m):
        return lax.ppermute(value, "dp", [(i, i ^ (m * inner)) for i in range(outer * inner)])

    def within(value, m):
        return lax.ppermute(value, "dp", [(i, i ^ m) for i in range(outer * inner)])

    def core_swap(value, q):
        return lax.ppermute(value, "expert", [(i, i ^ q) for i in range(pieces)])

    def choose(candidates):
        outs = pl.pallas_call(
            functools.partial(choose_body, inner, here),
            in_specs=[smem] + [vmem] * len(candidates),
            out_specs=[vmem] * (inner + 1),
            out_shape=chosen_shape,
            compiler_params=params,
            cost_estimate=cost(4 * plane * count * width, 6 * plane * width),
            name="choose",
        )(where, *candidates)
        tables.append(outs[-1])
        return outs[:-1]

    tables, owned = [own[-1]], []

    def spread(blocks):
        return [blocks[0]] + [within(blocks[m], m) for m in range(1, inner)]

    def share(arrived):
        mine = jnp.concatenate(arrived, axis=0).reshape(inner, here, CAP, 2 * width)
        owned.append([mine] + [core_swap(mine, q) for q in range(1, pieces)])

    def chained(blocks, arrived):
        sent, arrived = lax.optimization_barrier((blocks[1:], arrived))
        share(arrived)
        return [blocks[0]] + [within(sent[m - 1], m) for m in range(1, inner)]

    def held(values, arrived):
        values, arrived[1:] = lax.optimization_barrier((values, arrived[1:]))
        return values

    if outer == 4:
        middle = [(i, i ^ (3 * inner)) for i in range(inner, 3 * inner)]
        outward = [(i, i ^ inner) for i in range(inner, 3 * inner)]
        near = across(payload, 1)
        mid = lax.ppermute(payload, "dp", middle)
        first = spread(own[:-1])
        near, mid = held([near, mid], first)
        second = choose((near,))
        far = lax.ppermute(near, "dp", middle)
        out_mid = lax.ppermute(mid, "dp", outward)
        second = chained(second, first)
        far, out_mid = held([far, out_mid], second)
        third = choose((out_mid, far))
        out_far = lax.ppermute(far, "dp", outward)
        third = chained(third, second)
        fourth = choose((out_far, mid))
        fourth = chained(fourth, third)
        share(fourth)
    else:
        for m in range(outer):
            share(spread(choose((across(payload, m),)) if m else own[:-1]))

    rows_in = [owned[r][q] for q in range(pieces) for r in range(outer)]
    n_in = len(rows_in)
    lifted_spec = [pl.BlockSpec((inner, 1, CAP, width), lambda e: (0, e, 0, 0))] * n_in
    scaled_spec = [pl.BlockSpec((inner, 1, CAP, width), lambda e: (0, e, 0, 1))] * n_in
    weight_spec = pl.BlockSpec((1, hidden_width, features), lambda e: (e, 0, 0))
    unit_spec = pl.BlockSpec((1, hidden_width, line), lambda e: (e, 0, 0))
    weight_bytes = 2 * here * hidden_width * features
    row_bytes = 2 * here * line * features
    flops = 2 * here * line * hidden_width * features
    unit_shape = (here, hidden_width, line)
    back = pl.pallas_call(
        functools.partial(rows_body, outer, pieces),
        grid=(here,),
        in_specs=[smem] + lifted_spec + scaled_spec + [weight_spec, weight_spec],
        out_specs=[unit_spec, unit_spec] + lifted_spec,
        out_shape=[shape(unit_shape, BF16)] * 2 + [shape((inner, here, CAP, width), BF16)] * n_in,
        compiler_params=params,
        cost_estimate=cost(3 * flops, 2 * weight_bytes + 3 * row_bytes),
        name="rows",
    )(where, *rows_in, *rows_in, up_weight, down_weight)
    hidden, pre, partial = back[0], back[1], back[2:]
    any_place = pl.BlockSpec(memory_space=pl.ANY)

    def weight_grads(earlier):
        return pl.pallas_call(
            functools.partial(grads_body, outer, pieces),
            grid=(here,),
            in_specs=[smem] + lifted_spec + scaled_spec + [unit_spec, unit_spec, any_place],
            out_specs=[weight_spec, weight_spec, pl.BlockSpec((8, 128), lambda e: (0, 0))],
            out_shape=[shape(up_weight.shape, BF16)] * 2 + [shape((8, 128), F32)],
            compiler_params=params,
            cost_estimate=cost(2 * flops, 2 * weight_bytes + 2 * row_bytes),
            name="weight_grads",
        )(where, *rows_in, *rows_in, hidden, pre, earlier)

    def combine(group, blocks, earlier):
        return pl.pallas_call(
            functools.partial(combine_body, len(blocks), len(group)),
            in_specs=[vmem] * (len(group) + len(blocks)) + [any_place] * len(earlier),
            out_specs=[vmem] * len(group),
            out_shape=[shape((count, width), BF16 if r else F32) for r in group],
            compiler_params=params,
            cost_estimate=cost(2 * len(group) * plane * count * width, 2 * len(group) * plane * width),
            name="combine",
        )(*[tables[r] for r in group], *blocks, *earlier)

    swapped = [[core_swap(partial[q * outer + r], q) for q in range(1, pieces)] for r in range(outer)]
    groups = [list(g) for g in ([outer - 1], range(outer - 2, 0, -1), [0]) if len(g) and g[0] < outer]
    groups = groups if outer > 1 else [[0]]
    ready = []
    for group in groups:
        rows = []
        for r in group:
            total = partial[r].astype(F32)
            for value in swapped[r]:
                total = total + value.astype(F32)
            rows.append(total.astype(BF16).reshape(inner, part, width))
        ready.append([jnp.concatenate([row[m] for row in rows], axis=0) for m in range(inner)])
    sums, flag = [], []
    for i, group in enumerate(groups):
        blocks = [ready[i][0]] + [within(ready[i][m], m) for m in range(1, inner)]
        if i + 1 < len(groups):
            blocks[-1], ready[i + 1][1:] = lax.optimization_barrier((blocks[-1], ready[i + 1][1:]))
        if i == 1:
            grad_up, grad_down, flag = weight_grads(sent)
            flag = [flag]
        done = combine(group, blocks, flag)
        for r, value in zip(group, done):
            if r:
                sent = value
                sums.append(across(value, r))
            else:
                grad_tokens = value
    if not flag:
        grad_up, grad_down, _ = weight_grads(grad_tokens)
    for value in sums:
        grad_tokens = grad_tokens + value.astype(F32)
    return (grad_tokens, grad_up, grad_down)


def solution(mesh):
    in_specs = (
        P("dp", None),
        P("dp"),
        P(),
        P("dp", None),
        P("dp", None),
        P("dp", "expert", None),
        P("dp", "expert", None),
        P("dp", None),
    )
    out_specs = (P("dp", "expert"), P("dp", "expert", None), P("dp", "expert", None))
    return jax.shard_map(
        functools.partial(local, outer_extent(mesh)), mesh=mesh, in_specs=in_specs, out_specs=out_specs, check_vma=False
    )
```

```python
import functools

import jax
import jax.numpy as jnp
from jax import lax
from jax.experimental import pallas as pl
from jax.experimental.pallas import tpu as pltpu
from jax.sharding import PartitionSpec as P

EXPERTS = 64
TOPK = 6
CAP = 16
META = 16
F32 = jnp.float32
BF16 = jnp.bfloat16
VMEM_LIMIT = 32 << 20
SMALL_LIMIT = 8 << 20
PAYLOAD_LIMIT = 62 << 20
ROWS_LIMIT = 16 << 20


def outer_extent(mesh):
    line = list(mesh.devices.reshape(mesh.devices.shape[0], -1)[:, 0])
    total = len(line)
    block = 1
    coords = [getattr(device, "coords", None) for device in line]
    if all(c is not None for c in coords):
        for axis in range(len(coords[0])):
            run = 1
            while run < total and coords[run][axis] == coords[0][axis]:
                run += 1
            if run < total:
                block = max(block, run)
    if block == 1:
        while block * block < total:
            block *= 2
    return total // block


def dot(a, b, dims):
    return lax.dot_general(a, b, (dims, ((), ())), preferred_element_type=F32)


def payload_body(inner, experts_here, routes, gates, arms, tokens, cotangent, bias, out, *refs):
    rows_in, bias_in, sems = refs[inner + 1 :]
    dp_index = lax.axis_index("dp")
    where = [lax.axis_index("expert"), lax.div(dp_index, inner), lax.rem(dp_index, inner)]
    rows, width = rows_in.shape[1:]
    at = pl.multiple_of(where[0] * width, width)
    copies = [
        pltpu.make_async_copy(tokens.at[:, pl.ds(at, width)], rows_in.at[0], sems.at[0]),
        pltpu.make_async_copy(cotangent.at[:, pl.ds(at, width)], rows_in.at[1], sems.at[1]),
        pltpu.make_async_copy(bias.at[:, pl.ds(at, width)], bias_in, sems.at[2]),
    ]
    for copy in copies:
        copy.start()
    ids = lax.broadcasted_iota(jnp.int32, (bias.shape[0], rows), 0)
    pick = (ids == arms[...]).astype(F32).astype(BF16)
    out[2 * rows :, :] = jnp.zeros((META, width), BF16)
    table = [ref[...].astype(F32) for ref in (routes, gates)]
    rest = jnp.zeros((META - 2 * TOPK, rows), F32)
    out[2 * rows :, 0:rows] = jnp.concatenate(table + [rest], axis=0).astype(BF16)
    for copy in copies:
        copy.wait()
    lift = dot(pick, bias_in[...], ((0,), (0,)))
    out[0:rows, :] = (rows_in[0].astype(F32) + lift).astype(BF16)
    out[rows : 2 * rows, :] = rows_in[1]
    choose_body(inner, experts_here, 1, where, out, *refs[: inner + 1])


def choose_body(inner, experts_here, candidates, where, *refs):
    outs = refs[-(inner + 1) :]
    payloads = refs[:candidates]
    table_out = outs[-1]
    rows = (payloads[0].shape[0] - META) // 2
    width = payloads[0].shape[1]
    if len(payloads) == 1:
        load = lambda a, b, c, d: payloads[0][a:b, c:d]
    else:
        flag = where[3] == 1
        load = lambda a, b, c, d: jnp.where(flag, payloads[0][a:b, c:d], payloads[1][a:b, c:d])
    meta = load(2 * rows, 2 * rows + META, 0, rows).astype(F32)
    count = inner * experts_here
    line = lax.broadcasted_iota(jnp.int32, (count, rows), 0)
    owner = jnp.bitwise_xor(lax.div(line, experts_here), where[2])
    ids = ((where[1] * inner + owner) * experts_here + lax.rem(line, experts_here)).astype(F32)
    named = jnp.zeros((count, rows), F32)
    weight = jnp.zeros((count, rows), F32)
    for k in range(TOPK):
        hit = (ids == meta[k : k + 1, :]).astype(F32)
        named = named + hit
        weight = weight + hit * meta[TOPK + k : TOPK + k + 1, :]
    earlier = (
        lax.broadcasted_iota(jnp.int32, (rows, rows), 0) < lax.broadcasted_iota(jnp.int32, (rows, rows), 1)
    ).astype(F32)
    rank = dot(named.astype(BF16), earlier.astype(BF16), ((1,), (0,)))
    rank = jnp.where(named > 0, rank, -1.0)
    slot = lax.broadcasted_iota(jnp.int32, (count, CAP, rows), 1).astype(F32)
    here = slot == rank[:, None, :]
    table = jnp.where(here, 1.0, 0.0).reshape(count * CAP, rows).astype(BF16)
    scale = jnp.where(here, (weight * (1.0 / 64.0))[:, None, :], 0.0).reshape(count * CAP, rows).astype(BF16)
    table_out[...] = table
    lifted = dot(table, load(0, rows, 0, width), ((1,), (0,))).astype(BF16)
    scaled = dot(scale, load(rows, 2 * rows, 0, width), ((1,), (0,))).astype(BF16)
    part = experts_here * CAP
    for m in range(inner):
        outs[m][:, 0:width] = lifted[m * part : (m + 1) * part]
        outs[m][:, width : 2 * width] = scaled[m * part : (m + 1) * part]


def gathered(refs, *part):
    values = [ref[part] if part else ref[...] for ref in refs]
    return jnp.concatenate([value.reshape(-1, value.shape[-1]) for value in values], axis=0)


def rows_body(rounds, pieces, skipped, where, *refs):
    n = rounds * pieces
    xs = refs[:n]
    up, down = refs[n : n + 2]
    hidden_out, pre_out, *outs = refs[n + 2 + skipped :]
    width = outs[0].shape[-1]
    at = [pl.multiple_of(jnp.bitwise_xor(where[0], q) * width, width) for q in range(pieces)]

    def one(e):
        def project(weight, low):
            total = None
            for q in range(pieces):
                x = gathered(xs[q * rounds : (q + 1) * rounds], slice(None), e, slice(None), slice(low, low + width))
                term = dot(weight[e, :, pl.ds(at[q], width)], x, ((1,), (1,)))
                total = term if total is None else total + term
            return total

        preact = project(up, 0)
        backprop = project(down, width)
        s = 1.0 / (1.0 + jnp.exp(-preact))
        hidden_out[e] = (preact * s).astype(BF16)
        pre = (backprop * s * (1.0 + preact * (1.0 - s))).astype(BF16)
        pre_out[e] = pre
        turned = pre.T
        for q in range(pieces):
            part = dot(turned, up[e, :, pl.ds(at[q], width)], ((1,), (0,))).astype(BF16)
            each = part.shape[0] // rounds
            for r in range(rounds):
                ref = outs[q * rounds + r]
                ref[:, e, :, :] = part[r * each : (r + 1) * each].reshape(ref.shape[0], ref.shape[2], width)

    for e in range(up.shape[0]):
        one(e)


def grads_body(rounds, pieces, where, *refs):
    n = rounds * pieces
    hidden, pre, _, grad_up, grad_down, flag = refs[2 * n :]
    for unit, xs, grad in ((pre, refs[:n], grad_up), (hidden, refs[n : 2 * n], grad_down)):
        for q in range(pieces):
            width = xs[0].shape[-1]
            at = pl.multiple_of(jnp.bitwise_xor(where[0], q) * width, width)
            x = gathered(xs[q * rounds : (q + 1) * rounds])
            grad[0, :, pl.ds(at, width)] = dot(unit[0], x, ((1,), (0,))).astype(BF16)
    flag[...] = jnp.zeros(flag.shape, F32)


def touch_body(weight, _, out):
    out[...] = weight[0, 0:8, 0:128].astype(F32)


def combine_body(blocks, groups, *refs):
    tables, rows, outs = refs[:groups], refs[groups : groups + blocks], refs[-groups:]
    part = rows[0].shape[0] // groups
    for g in range(groups):
        mine = jnp.concatenate([ref[g * part : (g + 1) * part, :] for ref in rows], axis=0)
        outs[g][...] = dot(tables[g][...], mine, ((0,), (0,))).astype(outs[g].dtype)


def local(outer, tokens, arms, arm_bias, routes, gates, up_weight, down_weight, cotangent):
    count, features = tokens.shape
    here, hidden_width, _ = up_weight.shape
    inner = lax.axis_size("dp") // outer
    pieces = lax.axis_size("expert")
    width = features // pieces
    part = here * CAP
    plane = inner * part
    line = outer * inner * CAP
    dp_index = lax.axis_index("dp")
    core = lax.axis_index("expert")
    z_index = dp_index // inner
    edge = jnp.logical_or(z_index == 0, z_index == outer - 1)
    where = jnp.stack([core, z_index, dp_index % inner, edge.astype(jnp.int32)]).astype(jnp.int32)
    smem = pl.BlockSpec(memory_space=pltpu.SMEM)
    vmem = pl.BlockSpec(memory_space=pltpu.VMEM)
    params = pltpu.CompilerParams(vmem_limit_bytes=VMEM_LIMIT)
    shape = jax.ShapeDtypeStruct

    def cost(flops, moved):
        return pl.CostEstimate(flops=int(flops), bytes_accessed=int(moved), transcendentals=0)

    hbm = pl.BlockSpec(memory_space=pltpu.HBM)
    chosen_shape = [shape((part, 2 * width), BF16)] * inner + [shape((plane, count), BF16)]
    payload, *own = pl.pallas_call(
        functools.partial(payload_body, inner, here),
        in_specs=[vmem, vmem, vmem, hbm, hbm, hbm],
        out_specs=[vmem] * (inner + 2),
        out_shape=[shape((2 * count + META, width), BF16), *chosen_shape],
        scratch_shapes=[
            pltpu.VMEM((2, count, width), BF16),
            pltpu.VMEM((arm_bias.shape[0], width), BF16),
            pltpu.SemaphoreType.DMA((3,)),
        ],
        compiler_params=pltpu.CompilerParams(vmem_limit_bytes=PAYLOAD_LIMIT),
        name="payload",
    )(routes.T, gates.T, arms.reshape(1, count), tokens, cotangent, arm_bias)

    def across(value, m):
        return lax.ppermute(value, "dp", [(i, i ^ (m * inner)) for i in range(outer * inner)])

    def within(value, m):
        return lax.ppermute(value, "dp", [(i, i ^ m) for i in range(outer * inner)])

    def core_swap(value, q):
        return lax.ppermute(value, "expert", [(i, i ^ q) for i in range(pieces)])

    small = pltpu.CompilerParams(vmem_limit_bytes=SMALL_LIMIT)
    any_place = pl.BlockSpec(memory_space=pl.ANY)

    def choose(candidates, earlier=()):
        outs = pl.pallas_call(
            functools.partial(choose_body, inner, here, len(candidates)),
            in_specs=[smem] + [vmem] * len(candidates) + [any_place] * len(earlier),
            out_specs=[vmem] * (inner + 1),
            out_shape=chosen_shape,
            compiler_params=small,
            cost_estimate=cost(4 * plane * count * width, 6 * plane * width),
            name="choose",
        )(where, *candidates, *earlier)
        tables.append(outs[-1])
        return outs[:-1]

    def touch(weight, earlier):
        return pl.pallas_call(
            touch_body,
            in_specs=[vmem, any_place],
            out_specs=vmem,
            out_shape=shape((8, 128), F32),
            compiler_params=small,
            name="touch",
        )(weight, earlier)

    tables, owned = [own[-1]], []

    def spread(blocks):
        return [blocks[0]] + [within(blocks[m], m) for m in range(1, inner)]

    def share(arrived):
        mine = jnp.concatenate(arrived, axis=0).reshape(inner, here, CAP, 2 * width)
        owned.append([mine] + [core_swap(mine, q) for q in range(1, pieces)])

    def chained(blocks, arrived):
        sent, arrived = lax.optimization_barrier((blocks[1:], arrived))
        share(arrived)
        return [blocks[0]] + [within(sent[m - 1], m) for m in range(1, inner)]

    def held(values, arrived):
        values, arrived[1:] = lax.optimization_barrier((values, arrived[1:]))
        return values

    if outer == 4:
        middle = [(i, i ^ (3 * inner)) for i in range(inner, 3 * inner)]
        outward = [(i, i ^ inner) for i in range(inner, 3 * inner)]
        near = across(payload, 1)
        mid = lax.ppermute(payload, "dp", middle)
        first = spread(own[:-1])
        near, mid = held([near, mid], first)
        second = choose((near,))
        far = lax.ppermute(near, "dp", middle)
        out_mid = lax.ppermute(mid, "dp", outward)
        second = chained(second, first)
        far, out_mid = held([far, out_mid], second)
        third = choose((out_mid, far))
        up_flag = touch(up_weight, third[0])
        out_far = lax.ppermute(far, "dp", outward)
        third = chained(third, second)
        fourth = choose((out_far, mid), (up_flag,))
        down_flag = touch(down_weight, fourth[0])
        fourth = chained(fourth, third)
        fourth[-1], down_flag = lax.optimization_barrier((fourth[-1], down_flag))
        flags_in = [down_flag]
        share(fourth)
    else:
        for m in range(outer):
            share(spread(choose((across(payload, m),)) if m else own[:-1]))
        flags_in = []

    rows_in = [owned[r][q] for q in range(pieces) for r in range(outer)]
    n_in = len(rows_in)
    lifted_spec = [pl.BlockSpec((inner, 1, CAP, width), lambda e: (0, e, 0, 0))] * n_in
    scaled_spec = [pl.BlockSpec((inner, 1, CAP, width), lambda e: (0, e, 0, 1))] * n_in
    weight_spec = pl.BlockSpec((1, hidden_width, features), lambda e: (e, 0, 0))
    unit_spec = pl.BlockSpec((1, hidden_width, line), lambda e: (e, 0, 0))
    weight_bytes = 2 * here * hidden_width * features
    row_bytes = 2 * here * line * features
    flops = 2 * here * line * hidden_width * features
    unit_shape = (here, hidden_width, line)
    back = pl.pallas_call(
        functools.partial(rows_body, outer, pieces, len(flags_in)),
        in_specs=[smem] + [vmem] * (n_in + 2) + [any_place] * len(flags_in),
        out_specs=[vmem] * (n_in + 2),
        out_shape=[shape(unit_shape, BF16)] * 2 + [shape((inner, here, CAP, width), BF16)] * n_in,
        compiler_params=pltpu.CompilerParams(vmem_limit_bytes=ROWS_LIMIT),
        cost_estimate=cost(3 * flops, 2 * weight_bytes + 3 * row_bytes),
        name="rows",
    )(where, *rows_in, up_weight, down_weight, *flags_in)
    hidden, pre, partial = back[0], back[1], back[2:]
    def weight_grads(earlier):
        return pl.pallas_call(
            functools.partial(grads_body, outer, pieces),
            grid=(here,),
            in_specs=[smem] + lifted_spec + scaled_spec + [unit_spec, unit_spec, any_place],
            out_specs=[weight_spec, weight_spec, pl.BlockSpec((8, 128), lambda e: (0, 0))],
            out_shape=[shape(up_weight.shape, BF16)] * 2 + [shape((8, 128), F32)],
            compiler_params=params,
            cost_estimate=cost(2 * flops, 2 * weight_bytes + 2 * row_bytes),
            name="weight_grads",
        )(where, *rows_in, *rows_in, hidden, pre, earlier)

    def combine(group, blocks, earlier):
        return pl.pallas_call(
            functools.partial(combine_body, len(blocks), len(group)),
            in_specs=[vmem] * (len(group) + len(blocks)) + [any_place] * len(earlier),
            out_specs=[vmem] * len(group),
            out_shape=[shape((count, width), BF16 if r else F32) for r in group],
            compiler_params=params,
            cost_estimate=cost(2 * len(group) * plane * count * width, 2 * len(group) * plane * width),
            name="combine",
        )(*[tables[r] for r in group], *blocks, *earlier)

    swapped = [[core_swap(partial[q * outer + r], q) for q in range(1, pieces)] for r in range(outer)]
    groups = [list(g) for g in ([outer - 1], range(outer - 2, 0, -1), [0]) if len(g) and g[0] < outer]
    groups = groups if outer > 1 else [[0]]
    ready = []
    for group in groups:
        rows = []
        for r in group:
            total = partial[r].astype(F32)
            for value in swapped[r]:
                total = total + value.astype(F32)
            rows.append(total.astype(BF16).reshape(inner, part, width))
        ready.append([jnp.concatenate([row[m] for row in rows], axis=0) for m in range(inner)])
    sums, flag = [], []
    for i, group in enumerate(groups):
        blocks = [ready[i][0]] + [within(ready[i][m], m) for m in range(1, inner)]
        if i + 1 < len(groups):
            blocks[-1], ready[i + 1][1:] = lax.optimization_barrier((blocks[-1], ready[i + 1][1:]))
        if i == 1:
            grad_up, grad_down, flag = weight_grads(sent)
            flag = [flag]
        done = combine(group, blocks, flag)
        for r, value in zip(group, done):
            if r:
                sent = value
                sums.append(across(value, r))
            else:
                grad_tokens = value
    if not flag:
        grad_up, grad_down, _ = weight_grads(grad_tokens)
    for value in sums:
        grad_tokens = grad_tokens + value.astype(F32)
    return (grad_tokens, grad_up, grad_down)


def solution(mesh):
    in_specs = (
        P("dp", None),
        P("dp"),
        P(),
        P("dp", None),
        P("dp", None),
        P("dp", "expert", None),
        P("dp", "expert", None),
        P("dp", None),
    )
    out_specs = (P("dp", "expert"), P("dp", "expert", None), P("dp", "expert", None))
    return jax.shard_map(
        functools.partial(local, outer_extent(mesh)), mesh=mesh, in_specs=in_specs, out_specs=out_specs, check_vma=False
    )
```

```python
import functools

import jax
import jax.numpy as jnp
from jax import lax
from jax.experimental import pallas as pl
from jax.experimental.pallas import tpu as pltpu
from jax.sharding import PartitionSpec as P

EXPERTS = 64
TOPK = 6
CAP = 16
META = 16
F32 = jnp.float32
BF16 = jnp.bfloat16
VMEM_LIMIT = 32 << 20
SMALL_LIMIT = 8 << 20
SLOTS = 4
GRADS_LIMIT = 24 << 20
PAYLOAD_LIMIT = 62 << 20
ROWS_LIMIT = 16 << 20


def outer_extent(mesh):
    line = list(mesh.devices.reshape(mesh.devices.shape[0], -1)[:, 0])
    total = len(line)
    block = 1
    coords = [getattr(device, "coords", None) for device in line]
    if all(c is not None for c in coords):
        for axis in range(len(coords[0])):
            run = 1
            while run < total and coords[run][axis] == coords[0][axis]:
                run += 1
            if run < total:
                block = max(block, run)
    if block == 1:
        while block * block < total:
            block *= 2
    return total // block


def dot(a, b, dims):
    return lax.dot_general(a, b, (dims, ((), ())), preferred_element_type=F32)


def payload_body(inner, experts_here, routes, gates, arms, tokens, cotangent, bias, out, *refs):
    rows_in, bias_in, sems = refs[inner + 1 :]
    dp_index = lax.axis_index("dp")
    where = [lax.axis_index("expert"), lax.div(dp_index, inner), lax.rem(dp_index, inner)]
    rows, width = rows_in.shape[1:]
    at = pl.multiple_of(where[0] * width, width)
    copies = [
        pltpu.make_async_copy(tokens.at[:, pl.ds(at, width)], rows_in.at[0], sems.at[0]),
        pltpu.make_async_copy(cotangent.at[:, pl.ds(at, width)], rows_in.at[1], sems.at[1]),
        pltpu.make_async_copy(bias.at[:, pl.ds(at, width)], bias_in, sems.at[2]),
    ]
    for copy in copies:
        copy.start()
    ids = lax.broadcasted_iota(jnp.int32, (bias.shape[0], rows), 0)
    pick = (ids == arms[...]).astype(F32).astype(BF16)
    out[2 * rows :, :] = jnp.zeros((META, width), BF16)
    table = [ref[...].astype(F32) for ref in (routes, gates)]
    rest = jnp.zeros((META - 2 * TOPK, rows), F32)
    out[2 * rows :, 0:rows] = jnp.concatenate(table + [rest], axis=0).astype(BF16)
    for copy in copies:
        copy.wait()
    lift = dot(pick, bias_in[...], ((0,), (0,)))
    out[0:rows, :] = (rows_in[0].astype(F32) + lift).astype(BF16)
    out[rows : 2 * rows, :] = rows_in[1]
    choose_body(inner, experts_here, 1, where, out, *refs[: inner + 1])


def choose_body(inner, experts_here, candidates, where, *refs):
    outs = refs[-(inner + 1) :]
    payloads = refs[:candidates]
    table_out = outs[-1]
    rows = (payloads[0].shape[0] - META) // 2
    width = payloads[0].shape[1]
    if len(payloads) == 1:
        load = lambda a, b, c, d: payloads[0][a:b, c:d]
    else:
        flag = where[3] == 1
        load = lambda a, b, c, d: jnp.where(flag, payloads[0][a:b, c:d], payloads[1][a:b, c:d])
    meta = load(2 * rows, 2 * rows + META, 0, rows).astype(F32)
    count = inner * experts_here
    line = lax.broadcasted_iota(jnp.int32, (count, rows), 0)
    owner = jnp.bitwise_xor(lax.div(line, experts_here), where[2])
    ids = ((where[1] * inner + owner) * experts_here + lax.rem(line, experts_here)).astype(F32)
    named = jnp.zeros((count, rows), F32)
    weight = jnp.zeros((count, rows), F32)
    for k in range(TOPK):
        hit = (ids == meta[k : k + 1, :]).astype(F32)
        named = named + hit
        weight = weight + hit * meta[TOPK + k : TOPK + k + 1, :]
    earlier = (
        lax.broadcasted_iota(jnp.int32, (rows, rows), 0) < lax.broadcasted_iota(jnp.int32, (rows, rows), 1)
    ).astype(F32)
    rank = dot(named.astype(BF16), earlier.astype(BF16), ((1,), (0,)))
    rank = jnp.where(named > 0, rank, -1.0)
    slot = lax.broadcasted_iota(jnp.int32, (count, CAP, rows), 1).astype(F32)
    here = slot == rank[:, None, :]
    table = jnp.where(here, 1.0, 0.0).reshape(count * CAP, rows).astype(BF16)
    scale = jnp.where(here, (weight * (1.0 / 64.0))[:, None, :], 0.0).reshape(count * CAP, rows).astype(BF16)
    table_out[...] = table
    lifted = dot(table, load(0, rows, 0, width), ((1,), (0,))).astype(BF16)
    scaled = dot(scale, load(rows, 2 * rows, 0, width), ((1,), (0,))).astype(BF16)
    part = experts_here * CAP
    for m in range(inner):
        outs[m][:, 0:width] = lifted[m * part : (m + 1) * part]
        outs[m][:, width : 2 * width] = scaled[m * part : (m + 1) * part]


def gathered(refs, *part):
    values = [ref[part] if part else ref[...] for ref in refs]
    return jnp.concatenate([value.reshape(-1, value.shape[-1]) for value in values], axis=0)


def rows_body(rounds, pieces, skipped, where, *refs):
    n = rounds * pieces
    xs = refs[:n]
    up, down = refs[n : n + 2]
    hidden_out, pre_out, *outs = refs[n + 2 + skipped :]
    width = outs[0].shape[-1]
    at = [pl.multiple_of(jnp.bitwise_xor(where[0], q) * width, width) for q in range(pieces)]

    def one(e):
        def project(weight, low):
            total = None
            for q in range(pieces):
                x = gathered(xs[q * rounds : (q + 1) * rounds], slice(None), e, slice(None), slice(low, low + width))
                term = dot(weight[e, :, pl.ds(at[q], width)], x, ((1,), (1,)))
                total = term if total is None else total + term
            return total

        preact = project(up, 0)
        backprop = project(down, width)
        s = 1.0 / (1.0 + jnp.exp(-preact))
        hidden_out[e] = (preact * s).astype(BF16)
        pre = (backprop * s * (1.0 + preact * (1.0 - s))).astype(BF16)
        pre_out[e] = pre
        turned = pre.T
        for q in range(pieces):
            part = dot(turned, up[e, :, pl.ds(at[q], width)], ((1,), (0,))).astype(BF16)
            each = part.shape[0] // rounds
            for r in range(rounds):
                ref = outs[q * rounds + r]
                ref[:, e, :, :] = part[r * each : (r + 1) * each].reshape(ref.shape[0], ref.shape[2], width)

    for e in range(up.shape[0]):
        one(e)


def grads_body(rounds, pieces, where, *refs):
    n = rounds * pieces
    xs = refs[:n]
    hidden, pre, _, grad_up, grad_down, flag, slots, sems = refs[n:]
    width = xs[0].shape[-1] // 2
    at = [pl.multiple_of(jnp.bitwise_xor(where[0], q) * width, width) for q in range(pieces)]
    copies = []
    for e in range(pre.shape[0]):
        for unit, low, grad in ((pre, 0, grad_up), (hidden, width, grad_down)):
            slot = len(copies) % SLOTS
            if len(copies) >= SLOTS:
                copies[len(copies) - SLOTS].wait()
            for q in range(pieces):
                x = gathered(xs[q * rounds : (q + 1) * rounds], slice(None), e, slice(None), slice(low, low + width))
                slots[slot, :, pl.ds(at[q], width)] = dot(unit[e], x, ((1,), (0,))).astype(BF16)
            copies.append(pltpu.make_async_copy(slots.at[slot], grad.at[e], sems.at[slot]))
            copies[-1].start()
    flag[...] = jnp.zeros(flag.shape, F32)
    for copy in copies[-SLOTS:]:
        copy.wait()


def touch_body(weight, _, out):
    out[...] = weight[0, 0:8, 0:128].astype(F32)


def combine_body(blocks, groups, *refs):
    tables, rows, outs = refs[:groups], refs[groups : groups + blocks], refs[-groups:]
    part = rows[0].shape[0] // groups
    for g in range(groups):
        mine = jnp.concatenate([ref[g * part : (g + 1) * part, :] for ref in rows], axis=0)
        outs[g][...] = dot(tables[g][...], mine, ((0,), (0,))).astype(outs[g].dtype)


def local(outer, tokens, arms, arm_bias, routes, gates, up_weight, down_weight, cotangent):
    count, features = tokens.shape
    here, hidden_width, _ = up_weight.shape
    inner = lax.axis_size("dp") // outer
    pieces = lax.axis_size("expert")
    width = features // pieces
    part = here * CAP
    plane = inner * part
    line = outer * inner * CAP
    dp_index = lax.axis_index("dp")
    core = lax.axis_index("expert")
    z_index = dp_index // inner
    edge = jnp.logical_or(z_index == 0, z_index == outer - 1)
    where = jnp.stack([core, z_index, dp_index % inner, edge.astype(jnp.int32)]).astype(jnp.int32)
    smem = pl.BlockSpec(memory_space=pltpu.SMEM)
    vmem = pl.BlockSpec(memory_space=pltpu.VMEM)
    params = pltpu.CompilerParams(vmem_limit_bytes=VMEM_LIMIT)
    shape = jax.ShapeDtypeStruct

    def cost(flops, moved):
        return pl.CostEstimate(flops=int(flops), bytes_accessed=int(moved), transcendentals=0)

    hbm = pl.BlockSpec(memory_space=pltpu.HBM)
    chosen_shape = [shape((part, 2 * width), BF16)] * inner + [shape((plane, count), BF16)]
    payload, *own = pl.pallas_call(
        functools.partial(payload_body, inner, here),
        in_specs=[vmem, vmem, vmem, hbm, hbm, hbm],
        out_specs=[vmem] * (inner + 2),
        out_shape=[shape((2 * count + META, width), BF16), *chosen_shape],
        scratch_shapes=[
            pltpu.VMEM((2, count, width), BF16),
            pltpu.VMEM((arm_bias.shape[0], width), BF16),
            pltpu.SemaphoreType.DMA((3,)),
        ],
        compiler_params=pltpu.CompilerParams(vmem_limit_bytes=PAYLOAD_LIMIT),
        name="payload",
    )(routes.T, gates.T, arms.reshape(1, count), tokens, cotangent, arm_bias)

    def across(value, m):
        return lax.ppermute(value, "dp", [(i, i ^ (m * inner)) for i in range(outer * inner)])

    def within(value, m):
        return lax.ppermute(value, "dp", [(i, i ^ m) for i in range(outer * inner)])

    def core_swap(value, q):
        return lax.ppermute(value, "expert", [(i, i ^ q) for i in range(pieces)])

    small = pltpu.CompilerParams(vmem_limit_bytes=SMALL_LIMIT)
    any_place = pl.BlockSpec(memory_space=pl.ANY)

    def choose(candidates, earlier=()):
        outs = pl.pallas_call(
            functools.partial(choose_body, inner, here, len(candidates)),
            in_specs=[smem] + [vmem] * len(candidates) + [any_place] * len(earlier),
            out_specs=[vmem] * (inner + 1),
            out_shape=chosen_shape,
            compiler_params=small,
            cost_estimate=cost(4 * plane * count * width, 6 * plane * width),
            name="choose",
        )(where, *candidates, *earlier)
        tables.append(outs[-1])
        return outs[:-1]

    def touch(weight, earlier):
        return pl.pallas_call(
            touch_body,
            in_specs=[vmem, any_place],
            out_specs=vmem,
            out_shape=shape((8, 128), F32),
            compiler_params=small,
            name="touch",
        )(weight, earlier)

    tables, owned = [own[-1]], []

    def spread(blocks):
        return [blocks[0]] + [within(blocks[m], m) for m in range(1, inner)]

    def share(arrived):
        mine = jnp.concatenate(arrived, axis=0).reshape(inner, here, CAP, 2 * width)
        owned.append([mine] + [core_swap(mine, q) for q in range(1, pieces)])

    def chained(blocks, arrived):
        sent, arrived = lax.optimization_barrier((blocks[1:], arrived))
        share(arrived)
        return [blocks[0]] + [within(sent[m - 1], m) for m in range(1, inner)]

    def held(values, arrived):
        values, arrived[1:] = lax.optimization_barrier((values, arrived[1:]))
        return values

    if outer == 4:
        middle = [(i, i ^ (3 * inner)) for i in range(inner, 3 * inner)]
        outward = [(i, i ^ inner) for i in range(inner, 3 * inner)]
        near = across(payload, 1)
        mid = lax.ppermute(payload, "dp", middle)
        first = spread(own[:-1])
        near, mid = held([near, mid], first)
        second = choose((near,))
        far = lax.ppermute(near, "dp", middle)
        out_mid = lax.ppermute(mid, "dp", outward)
        second = chained(second, first)
        far, out_mid = held([far, out_mid], second)
        third = choose((out_mid, far))
        up_flag = touch(up_weight, third[0])
        out_far = lax.ppermute(far, "dp", outward)
        third = chained(third, second)
        fourth = choose((out_far, mid), (up_flag,))
        down_flag = touch(down_weight, fourth[0])
        fourth = chained(fourth, third)
        fourth[-1], down_flag = lax.optimization_barrier((fourth[-1], down_flag))
        flags_in = [down_flag]
        share(fourth)
    else:
        for m in range(outer):
            share(spread(choose((across(payload, m),)) if m else own[:-1]))
        flags_in = []

    rows_in = [owned[r][q] for q in range(pieces) for r in range(outer)]
    n_in = len(rows_in)
    lifted_spec = [pl.BlockSpec((inner, 1, CAP, width), lambda e: (0, e, 0, 0))] * n_in
    scaled_spec = [pl.BlockSpec((inner, 1, CAP, width), lambda e: (0, e, 0, 1))] * n_in
    weight_spec = pl.BlockSpec((1, hidden_width, features), lambda e: (e, 0, 0))
    unit_spec = pl.BlockSpec((1, hidden_width, line), lambda e: (e, 0, 0))
    weight_bytes = 2 * here * hidden_width * features
    row_bytes = 2 * here * line * features
    flops = 2 * here * line * hidden_width * features
    unit_shape = (here, hidden_width, line)
    back = pl.pallas_call(
        functools.partial(rows_body, outer, pieces, len(flags_in)),
        in_specs=[smem] + [vmem] * (n_in + 2) + [any_place] * len(flags_in),
        out_specs=[vmem] * (n_in + 2),
        out_shape=[shape(unit_shape, BF16)] * 2 + [shape((inner, here, CAP, width), BF16)] * n_in,
        compiler_params=pltpu.CompilerParams(vmem_limit_bytes=ROWS_LIMIT),
        cost_estimate=cost(3 * flops, 2 * weight_bytes + 3 * row_bytes),
        name="rows",
    )(where, *rows_in, up_weight, down_weight, *flags_in)
    hidden, pre, partial = back[0], back[1], back[2:]
    def weight_grads(earlier):
        return pl.pallas_call(
            functools.partial(grads_body, outer, pieces),
            in_specs=[smem] + [vmem] * (n_in + 2) + [any_place],
            out_specs=[hbm, hbm, vmem],
            out_shape=[shape(up_weight.shape, BF16)] * 2 + [shape((8, 128), F32)],
            scratch_shapes=[pltpu.VMEM((SLOTS, hidden_width, features), BF16), pltpu.SemaphoreType.DMA((SLOTS,))],
            compiler_params=pltpu.CompilerParams(vmem_limit_bytes=GRADS_LIMIT),
            cost_estimate=cost(2 * flops, 2 * weight_bytes + 2 * row_bytes),
            name="weight_grads",
        )(where, *rows_in, hidden, pre, earlier)

    def combine(group, blocks, earlier):
        return pl.pallas_call(
            functools.partial(combine_body, len(blocks), len(group)),
            in_specs=[vmem] * (len(group) + len(blocks)) + [any_place] * len(earlier),
            out_specs=[vmem] * len(group),
            out_shape=[shape((count, width), BF16 if r else F32) for r in group],
            compiler_params=params,
            cost_estimate=cost(2 * len(group) * plane * count * width, 2 * len(group) * plane * width),
            name="combine",
        )(*[tables[r] for r in group], *blocks, *earlier)

    swapped = [[core_swap(partial[q * outer + r], q) for q in range(1, pieces)] for r in range(outer)]
    groups = [list(g) for g in ([outer - 1], range(outer - 2, 0, -1), [0]) if len(g) and g[0] < outer]
    groups = groups if outer > 1 else [[0]]
    ready = []
    for group in groups:
        rows = []
        for r in group:
            total = partial[r].astype(F32)
            for value in swapped[r]:
                total = total + value.astype(F32)
            rows.append(total.astype(BF16).reshape(inner, part, width))
        ready.append([jnp.concatenate([row[m] for row in rows], axis=0) for m in range(inner)])
    sums, flag = [], []
    for i, group in enumerate(groups):
        blocks = [ready[i][0]] + [within(ready[i][m], m) for m in range(1, inner)]
        if i + 1 < len(groups):
            blocks[-1], ready[i + 1][1:] = lax.optimization_barrier((blocks[-1], ready[i + 1][1:]))
        if i == 1:
            grad_up, grad_down, flag = weight_grads(sent)
            flag = [flag]
        done = combine(group, blocks, flag)
        for r, value in zip(group, done):
            if r:
                sent = value
                sums.append(across(value, r))
            else:
                grad_tokens = value
    if not flag:
        grad_up, grad_down, _ = weight_grads(grad_tokens)
    for value in sums:
        grad_tokens = grad_tokens + value.astype(F32)
    return (grad_tokens, grad_up, grad_down)


def solution(mesh):
    in_specs = (
        P("dp", None),
        P("dp"),
        P(),
        P("dp", None),
        P("dp", None),
        P("dp", "expert", None),
        P("dp", "expert", None),
        P("dp", None),
    )
    out_specs = (P("dp", "expert"), P("dp", "expert", None), P("dp", "expert", None))
    return jax.shard_map(
        functools.partial(local, outer_extent(mesh)), mesh=mesh, in_specs=in_specs, out_specs=out_specs, check_vma=False
    )
```

```python
import functools

import jax
import jax.numpy as jnp
from jax import lax
from jax.experimental import pallas as pl
from jax.experimental.pallas import tpu as pltpu
from jax.sharding import PartitionSpec as P

EXPERTS = 64
TOPK = 6
CAP = 16
META = 16
F32 = jnp.float32
BF16 = jnp.bfloat16
VMEM_LIMIT = 32 << 20
SMALL_LIMIT = 8 << 20
SLOTS = 4
GRADS_LIMIT = 24 << 20
PAYLOAD_LIMIT = 62 << 20
ROWS_LIMIT = 16 << 20


def outer_extent(mesh):
    line = list(mesh.devices.reshape(mesh.devices.shape[0], -1)[:, 0])
    total = len(line)
    block = 1
    coords = [getattr(device, "coords", None) for device in line]
    if all(c is not None for c in coords):
        for axis in range(len(coords[0])):
            run = 1
            while run < total and coords[run][axis] == coords[0][axis]:
                run += 1
            if run < total:
                block = max(block, run)
    if block == 1:
        while block * block < total:
            block *= 2
    return total // block


def dot(a, b, dims):
    return lax.dot_general(a, b, (dims, ((), ())), preferred_element_type=F32)


def payload_body(inner, experts_here, routes, gates, arms, tokens, cotangent, bias, out, *refs):
    rows_in, bias_in, sems = refs[inner + 1 :]
    dp_index = lax.axis_index("dp")
    where = [lax.axis_index("expert"), lax.div(dp_index, inner), lax.rem(dp_index, inner)]
    rows, width = rows_in.shape[1:]
    at = pl.multiple_of(where[0] * width, width)
    copies = [
        pltpu.make_async_copy(tokens.at[:, pl.ds(at, width)], rows_in.at[0], sems.at[0]),
        pltpu.make_async_copy(cotangent.at[:, pl.ds(at, width)], rows_in.at[1], sems.at[1]),
        pltpu.make_async_copy(bias.at[:, pl.ds(at, width)], bias_in, sems.at[2]),
    ]
    for copy in copies:
        copy.start()
    ids = lax.broadcasted_iota(jnp.int32, (bias.shape[0], rows), 0)
    pick = (ids == arms[...]).astype(F32).astype(BF16)
    out[2 * rows :, :] = jnp.zeros((META, width), BF16)
    table = [ref[...].astype(F32) for ref in (routes, gates)]
    rest = jnp.zeros((META - 2 * TOPK, rows), F32)
    out[2 * rows :, 0:rows] = jnp.concatenate(table + [rest], axis=0).astype(BF16)
    for copy in copies:
        copy.wait()
    lift = dot(pick, bias_in[...], ((0,), (0,)))
    out[0:rows, :] = (rows_in[0].astype(F32) + lift).astype(BF16)
    out[rows : 2 * rows, :] = rows_in[1]
    choose_body(inner, experts_here, 1, where, out, *refs[: inner + 1])


def choose_body(inner, experts_here, candidates, where, *refs):
    outs = refs[-(inner + 1) :]
    payloads = refs[:candidates]
    table_out = outs[-1]
    rows = (payloads[0].shape[0] - META) // 2
    width = payloads[0].shape[1]
    if len(payloads) == 1:
        load = lambda a, b, c, d: payloads[0][a:b, c:d]
    else:
        flag = where[3] == 1
        load = lambda a, b, c, d: jnp.where(flag, payloads[0][a:b, c:d], payloads[1][a:b, c:d])
    meta = load(2 * rows, 2 * rows + META, 0, rows).astype(F32)
    count = inner * experts_here
    line = lax.broadcasted_iota(jnp.int32, (count, rows), 0)
    owner = jnp.bitwise_xor(lax.div(line, experts_here), where[2])
    ids = ((where[1] * inner + owner) * experts_here + lax.rem(line, experts_here)).astype(F32)
    named = jnp.zeros((count, rows), F32)
    weight = jnp.zeros((count, rows), F32)
    for k in range(TOPK):
        hit = (ids == meta[k : k + 1, :]).astype(F32)
        named = named + hit
        weight = weight + hit * meta[TOPK + k : TOPK + k + 1, :]
    earlier = (
        lax.broadcasted_iota(jnp.int32, (rows, rows), 0) < lax.broadcasted_iota(jnp.int32, (rows, rows), 1)
    ).astype(F32)
    rank = dot(named.astype(BF16), earlier.astype(BF16), ((1,), (0,)))
    rank = jnp.where(named > 0, rank, -1.0)
    slot = lax.broadcasted_iota(jnp.int32, (count, CAP, rows), 1).astype(F32)
    here = slot == rank[:, None, :]
    table = jnp.where(here, 1.0, 0.0).reshape(count * CAP, rows).astype(BF16)
    scale = jnp.where(here, (weight * (1.0 / 64.0))[:, None, :], 0.0).reshape(count * CAP, rows).astype(BF16)
    table_out[...] = table
    lifted = dot(table, load(0, rows, 0, width), ((1,), (0,))).astype(BF16)
    scaled = dot(scale, load(rows, 2 * rows, 0, width), ((1,), (0,))).astype(BF16)
    part = experts_here * CAP
    for m in range(inner):
        outs[m][:, 0:width] = lifted[m * part : (m + 1) * part]
        outs[m][:, width : 2 * width] = scaled[m * part : (m + 1) * part]


def gathered(refs, *part):
    values = [ref[part] if part else ref[...] for ref in refs]
    return jnp.concatenate([value.reshape(-1, value.shape[-1]) for value in values], axis=0)


def rows_body(rounds, pieces, skipped, where, *refs):
    n = rounds * pieces
    xs = refs[:n]
    up, down = refs[n : n + 2]
    hidden_out, pre_out, *outs = refs[n + 2 + skipped :]
    width = outs[0].shape[-1]
    at = [pl.multiple_of(jnp.bitwise_xor(where[0], q) * width, width) for q in range(pieces)]

    def one(e):
        def project(weight, low):
            total = None
            for q in range(pieces):
                x = gathered(xs[q * rounds : (q + 1) * rounds], slice(None), e, slice(None), slice(low, low + width))
                term = dot(weight[e, :, pl.ds(at[q], width)], x, ((1,), (1,)))
                total = term if total is None else total + term
            return total

        preact = project(up, 0)
        backprop = project(down, width)
        s = 1.0 / (1.0 + jnp.exp(-preact))
        hidden_out[e] = (preact * s).astype(BF16)
        pre = (backprop * s * (1.0 + preact * (1.0 - s))).astype(BF16)
        pre_out[e] = pre
        turned = pre.T
        for q in range(pieces):
            part = dot(turned, up[e, :, pl.ds(at[q], width)], ((1,), (0,))).astype(BF16)
            each = part.shape[0] // rounds
            for r in range(rounds):
                ref = outs[q * rounds + r]
                ref[:, e, :, :] = part[r * each : (r + 1) * each].reshape(ref.shape[0], ref.shape[2], width)

    for e in range(up.shape[0]):
        one(e)


def grads_body(rounds, pieces, where, *refs):
    n = rounds * pieces
    xs = refs[:n]
    hidden, pre, _, grad_up, grad_down, flag, slots, sems = refs[n:]
    width = xs[0].shape[-1] // 2
    at = [pl.multiple_of(jnp.bitwise_xor(where[0], q) * width, width) for q in range(pieces)]
    copies = []
    for e in range(pre.shape[0]):
        for unit, low, grad in ((pre, 0, grad_up), (hidden, width, grad_down)):
            slot = len(copies) % SLOTS
            if len(copies) >= SLOTS:
                copies[len(copies) - SLOTS].wait()
            for q in range(pieces):
                x = gathered(xs[q * rounds : (q + 1) * rounds], slice(None), e, slice(None), slice(low, low + width))
                slots[slot, :, pl.ds(at[q], width)] = dot(unit[e], x, ((1,), (0,))).astype(BF16)
            copies.append(pltpu.make_async_copy(slots.at[slot], grad.at[e], sems.at[slot]))
            copies[-1].start()
    flag[...] = jnp.zeros(flag.shape, F32)
    for copy in copies[-SLOTS:]:
        copy.wait()


def touch_body(weight, _, out):
    out[...] = weight[0, 0:8, 0:128].astype(F32)


def combine_body(blocks, groups, *refs):
    tables, rows, outs = refs[:groups], refs[groups : groups + blocks], refs[-groups:]
    part = rows[0].shape[0] // groups
    for g in range(groups):
        mine = jnp.concatenate([ref[g * part : (g + 1) * part, :] for ref in rows], axis=0)
        outs[g][...] = dot(tables[g][...], mine, ((0,), (0,))).astype(outs[g].dtype)


def local(outer, tokens, arms, arm_bias, routes, gates, up_weight, down_weight, cotangent):
    count, features = tokens.shape
    here, hidden_width, _ = up_weight.shape
    inner = lax.axis_size("dp") // outer
    pieces = lax.axis_size("expert")
    width = features // pieces
    part = here * CAP
    plane = inner * part
    line = outer * inner * CAP
    dp_index = lax.axis_index("dp")
    core = lax.axis_index("expert")
    z_index = dp_index // inner
    edge = jnp.logical_or(z_index == 0, z_index == outer - 1)
    where = jnp.stack([core, z_index, dp_index % inner, edge.astype(jnp.int32)]).astype(jnp.int32)
    smem = pl.BlockSpec(memory_space=pltpu.SMEM)
    vmem = pl.BlockSpec(memory_space=pltpu.VMEM)
    params = pltpu.CompilerParams(vmem_limit_bytes=VMEM_LIMIT)
    shape = jax.ShapeDtypeStruct

    def cost(flops, moved):
        return pl.CostEstimate(flops=int(flops), bytes_accessed=int(moved), transcendentals=0)

    hbm = pl.BlockSpec(memory_space=pltpu.HBM)
    chosen_shape = [shape((part, 2 * width), BF16)] * inner + [shape((plane, count), BF16)]
    payload, *own = pl.pallas_call(
        functools.partial(payload_body, inner, here),
        in_specs=[vmem, vmem, vmem, hbm, hbm, hbm],
        out_specs=[vmem] * (inner + 2),
        out_shape=[shape((2 * count + META, width), BF16), *chosen_shape],
        scratch_shapes=[
            pltpu.VMEM((2, count, width), BF16),
            pltpu.VMEM((arm_bias.shape[0], width), BF16),
            pltpu.SemaphoreType.DMA((3,)),
        ],
        compiler_params=pltpu.CompilerParams(vmem_limit_bytes=PAYLOAD_LIMIT),
        name="payload",
    )(routes.T, gates.T, arms.reshape(1, count), tokens, cotangent, arm_bias)

    def across(value, m):
        return lax.ppermute(value, "dp", [(i, i ^ (m * inner)) for i in range(outer * inner)])

    def within(value, m):
        return lax.ppermute(value, "dp", [(i, i ^ m) for i in range(outer * inner)])

    def core_swap(value, q):
        return lax.ppermute(value, "expert", [(i, i ^ q) for i in range(pieces)])

    small = pltpu.CompilerParams(vmem_limit_bytes=SMALL_LIMIT)
    any_place = pl.BlockSpec(memory_space=pl.ANY)

    def choose(candidates, earlier=()):
        outs = pl.pallas_call(
            functools.partial(choose_body, inner, here, len(candidates)),
            in_specs=[smem] + [vmem] * len(candidates) + [any_place] * len(earlier),
            out_specs=[vmem] * (inner + 1),
            out_shape=chosen_shape,
            compiler_params=small,
            cost_estimate=cost(4 * plane * count * width, 6 * plane * width),
            name="choose",
        )(where, *candidates, *earlier)
        tables.append(outs[-1])
        return outs[:-1]

    def touch(weight, earlier):
        return pl.pallas_call(
            touch_body,
            in_specs=[vmem, any_place],
            out_specs=vmem,
            out_shape=shape((8, 128), F32),
            compiler_params=small,
            name="touch",
        )(weight, earlier)

    tables, owned = [own[-1]], []

    def spread(blocks):
        return [blocks[0]] + [within(blocks[m], m) for m in range(1, inner)]

    def share(arrived):
        mine = jnp.concatenate(arrived, axis=0).reshape(inner, here, CAP, 2 * width)
        owned.append([mine] + [core_swap(mine, q) for q in range(1, pieces)])

    def chained(blocks, arrived):
        sent, arrived = lax.optimization_barrier((blocks[1:], arrived))
        share(arrived)
        return [blocks[0]] + [within(sent[m - 1], m) for m in range(1, inner)]

    def held(values, arrived):
        values, arrived[1:] = lax.optimization_barrier((values, arrived[1:]))
        return values

    if outer == 4:
        middle = [(i, i ^ (3 * inner)) for i in range(inner, 3 * inner)]
        outward = [(i, i ^ inner) for i in range(inner, 3 * inner)]
        near = across(payload, 1)
        mid = lax.ppermute(payload, "dp", middle)
        first = spread(own[:-1])
        near, mid = held([near, mid], first)
        second = choose((near,))
        far = lax.ppermute(near, "dp", middle)
        out_mid = lax.ppermute(mid, "dp", outward)
        second = chained(second, first)
        far, out_mid = held([far, out_mid], second)
        third = choose((out_mid, far))
        up_flag = touch(up_weight, third[0])
        out_far = lax.ppermute(far, "dp", outward)
        third = chained(third, second)
        fourth = choose((out_far, mid), (up_flag,))
        down_flag = touch(down_weight, fourth[0])
        fourth = chained(fourth, third)
        fourth[-1], down_flag = lax.optimization_barrier((fourth[-1], down_flag))
        flags_in = [down_flag]
        share(fourth)
    else:
        for m in range(outer):
            share(spread(choose((across(payload, m),)) if m else own[:-1]))
        flags_in = []

    rows_in = [owned[r][q] for q in range(pieces) for r in range(outer)]
    n_in = len(rows_in)
    lifted_spec = [pl.BlockSpec((inner, 1, CAP, width), lambda e: (0, e, 0, 0))] * n_in
    scaled_spec = [pl.BlockSpec((inner, 1, CAP, width), lambda e: (0, e, 0, 1))] * n_in
    weight_spec = pl.BlockSpec((1, hidden_width, features), lambda e: (e, 0, 0))
    unit_spec = pl.BlockSpec((1, hidden_width, line), lambda e: (e, 0, 0))
    weight_bytes = 2 * here * hidden_width * features
    row_bytes = 2 * here * line * features
    flops = 2 * here * line * hidden_width * features
    unit_shape = (here, hidden_width, line)
    back = pl.pallas_call(
        functools.partial(rows_body, outer, pieces, len(flags_in)),
        in_specs=[smem] + [vmem] * (n_in + 2) + [any_place] * len(flags_in),
        out_specs=[vmem] * (n_in + 2),
        out_shape=[shape(unit_shape, BF16)] * 2 + [shape((inner, here, CAP, width), BF16)] * n_in,
        compiler_params=pltpu.CompilerParams(vmem_limit_bytes=ROWS_LIMIT),
        cost_estimate=cost(3 * flops, 2 * weight_bytes + 3 * row_bytes),
        name="rows",
    )(where, *rows_in, up_weight, down_weight, *flags_in)
    hidden, pre, partial = back[0], back[1], back[2:]
    def weight_grads(earlier):
        return pl.pallas_call(
            functools.partial(grads_body, outer, pieces),
            in_specs=[smem] + [vmem] * (n_in + 2) + [any_place],
            out_specs=[hbm, hbm, vmem],
            out_shape=[shape(up_weight.shape, BF16)] * 2 + [shape((8, 128), F32)],
            scratch_shapes=[pltpu.VMEM((SLOTS, hidden_width, features), BF16), pltpu.SemaphoreType.DMA((SLOTS,))],
            compiler_params=pltpu.CompilerParams(vmem_limit_bytes=GRADS_LIMIT),
            cost_estimate=cost(2 * flops, 2 * weight_bytes + 2 * row_bytes),
            name="weight_grads",
        )(where, *rows_in, hidden, pre, earlier)

    def combine(group, blocks, earlier):
        return pl.pallas_call(
            functools.partial(combine_body, len(blocks), len(group)),
            in_specs=[vmem] * (len(group) + len(blocks)) + [any_place] * len(earlier),
            out_specs=[vmem] * len(group),
            out_shape=[shape((count, width), BF16 if r else F32) for r in group],
            compiler_params=params,
            cost_estimate=cost(2 * len(group) * plane * count * width, 2 * len(group) * plane * width),
            name="combine",
        )(*[tables[r] for r in group], *blocks, *earlier)

    swapped = [[core_swap(partial[q * outer + r], q) for q in range(1, pieces)] for r in range(outer)]
    groups = [list(g) for g in ([outer - 1], range(outer - 2, 0, -1), [0]) if len(g) and g[0] < outer]
    groups = groups if outer > 1 else [[0]]
    ready = []
    for group in groups:
        rows = []
        for r in group:
            total = partial[r].astype(F32)
            for value in swapped[r]:
                total = total + value.astype(F32)
            rows.append(total.astype(BF16).reshape(inner, part, width))
        ready.append([jnp.concatenate([row[m] for row in rows], axis=0) for m in range(inner)])
    sums, flag = [], []
    for i, group in enumerate(groups):
        blocks = [ready[i][0]] + [within(ready[i][m], m) for m in range(1, inner)]
        if i == 1:
            grad_up, grad_down, flag = weight_grads(sent)
            flag = [flag]
        done = combine(group, blocks, flag)
        if i + 1 < len(groups):
            done, ready[i + 1][1:] = lax.optimization_barrier((done, ready[i + 1][1:]))
        for r, value in zip(group, done):
            if r:
                sent = value
                sums.append(across(value, r))
            else:
                grad_tokens = value
    if not flag:
        grad_up, grad_down, _ = weight_grads(grad_tokens)
    for value in sums:
        grad_tokens = grad_tokens + value.astype(F32)
    return (grad_tokens, grad_up, grad_down)


def solution(mesh):
    in_specs = (
        P("dp", None),
        P("dp"),
        P(),
        P("dp", None),
        P("dp", None),
        P("dp", "expert", None),
        P("dp", "expert", None),
        P("dp", None),
    )
    out_specs = (P("dp", "expert"), P("dp", "expert", None), P("dp", "expert", None))
    return jax.shard_map(
        functools.partial(local, outer_extent(mesh)), mesh=mesh, in_specs=in_specs, out_specs=out_specs, check_vma=False
    )
```
